32 devices in a mesh: rep: 2 (over y), dp: 4 (over z), fsdp: 2 (over x), tp: 2 (over core).
Axes of the slice: x: 2, y: 2, z: 4, core: 2. Of those that a mesh axis runs over, the one named last changes fastest.
Arguments:
- tokens: bfloat16 [4096, 8192], P(('rep', 'dp', 'fsdp'), 'tp'), parts along dimension 0, may hold values from -6 to 6
- output_gradient: bfloat16 [4096, 512], P(('rep', 'dp', 'fsdp')), parts along dimension 0, may hold values from -6 to 6
- frozen_value_weight: bfloat16 [8192, 512], P('tp', 'fsdp'), may hold values from -0.0625 to 0.0625
- adapter_down_weight: bfloat16 [32, 16, 8192], P(('rep', 'dp'), None, 'tp'), parts along dimension 0, may hold values from -0.0625 to 0.0625
- adapter_up_weight: bfloat16 [32, 16, 512], P(('rep', 'dp'), None, 'tp'), parts along dimension 0, may hold values from -0.25 to 0.25
- deal: int32 [4096, 1], P(('rep', 'dp', 'fsdp')), parts along dimension 0, may hold values from 0 to 3; in each aligned block of 256 rows (0 to 255, 256 to 511, ...) at most 80 rows name the same one
- row_local_job: int32 [4096], P(('rep', 'dp', 'fsdp')), parts along dimension 0, may hold values from 0 to 3
Outputs:
- value_output: bfloat16 [4096, 512], P(('rep', 'dp', 'fsdp'), 'tp'), parts along dimension 0
- input_gradient: bfloat16 [4096, 8192], P(('rep', 'dp', 'fsdp'), 'tp'), parts along dimension 0
- down_weight_gradient: float32 [32, 16, 8192], P(('rep', 'dp'), 'fsdp', 'tp'), parts along dimension 0
- up_weight_gradient: float32 [32, 16, 512], P(('rep', 'dp'), 'fsdp', 'tp'), parts along dimension 0
The draws below stay inside these ranges and needn't reach their ends.
There are 2 independent parts, one for each index of `rep`. The reference program is written for one: setup_inputs(seed, part) draws one part's arguments, and reference() takes and returns one part's arrays. A program takes and returns all parts, laid end to end along the dimension named above; an argument that names none is the same for every part. Nothing has to cross between parts.
Inputs may be any that keep to these rules, and one draw needn't show every extreme that they name: `deal`: within the rows of one device (aligned blocks of 256 rows) no index is named by more than 80 rows, and in some block one index is named exactly 80 times.
All inputs are finite; a program needn't handle non-finite values.
Results may differ from the reference program's by a relative error of at most 0.0034.
Values may be sent and summed in bfloat16 or wider, within the bound.
No kernel may reach another device: no remote copies, remote signals or barrier semaphores. Data moves between devices by JAX's collectives and lax.ppermute only.
A program may use at most 64 MiB of HBM per device.

```python
import math
import jax
import jax.numpy as jnp
import numpy as np
from jax import lax

MODEL_WIDTH = 8192
VALUE_WIDTH = 512
ADAPTER_RANK = 16
JOB_DEV = 4
ROWS_DEV = 256
ADAPTER_JOBS = 16
MOST = 80
TOKEN_ROWS = 2048
N_DP = 4


def touch_ends(values, own_key, smallest, largest):
    extent = values.shape
    spot = [jax.random.randint(jax.random.fold_in(own_key, axis), (), 0, extent[axis]) for axis in range(len(extent))]
    values = values.at[tuple(spot)].set(smallest)
    longest = extent.index(max(extent))
    spot[longest] = (spot[longest] + 1) % extent[longest]
    return values.at[tuple(spot)].set(largest)


def steps_of(key, dims, shards, least, top_value):
    loudness, own = 1.0, jax.random.fold_in(key, 6)
    for dim, blocks in shards:
        heights = jnp.exp(jax.random.uniform(jax.random.fold_in(own, dim), (blocks,), jnp.float32, least / len(shards), top_value / len(shards)))
        loudness = loudness * jnp.repeat(heights, dims[dim] // blocks).reshape([-1 if axis == dim else 1 for axis in range(len(dims))])
    return loudness


def assign_block(key, own, number, rows, amount, top, reach, skew):
    sequence = jax.random.permutation(key, amount)
    packed, usual = portions_of(amount, rows * top, reach, skew, True), portions_of(amount, rows * top, reach, skew, False)
    places = jnp.arange(amount)

    def named(lengths, turn):
        used = int((lengths > 0).sum())
        fixed = max(1, used // 4)
        shifted = fixed + (places - fixed + turn * (used - fixed)) % max(1, amount - fixed)
        return jnp.zeros((amount,), jnp.int32).at[sequence[jnp.where(places < fixed, places, shifted)]].set(jnp.asarray(lengths, jnp.int32))

    lengths = jnp.where(number % 4 == 0, named(packed, number // 4), named(usual, number - number // 4 - 1))
    mixed = jax.random.permutation(jax.random.fold_in(own, 3), amount)
    donor, taker = mixed[0:amount // 2 * 2:2], mixed[1:amount // 2 * 2:2]
    room = jnp.minimum(lengths[donor] - 1, reach - lengths[taker]) // 2
    room = jnp.where((donor == sequence[0]) | (taker == sequence[0]) | (lengths[taker] == 0), 0, jnp.maximum(room, 0))
    shifted = jax.random.randint(jax.random.fold_in(own, 4), (amount // 2,), 0, 1 << 20) % (room + 1)
    lengths = lengths.at[donor].add(-shifted).at[taker].add(shifted)
    labels = jnp.searchsorted(jnp.cumsum(lengths), jnp.arange(rows * top), side="right").astype(jnp.int32)
    grid = labels.reshape(top, rows).T
    grid = grid[jax.random.permutation(jax.random.fold_in(own, 1), rows)]
    turn = jax.random.randint(jax.random.fold_in(own, 2), (rows, 1), 0, top)
    return jnp.take_along_axis(grid, (jnp.arange(top)[None, :] + turn) % top, axis=1)


def portions_of(count, total, limit, skew, full):
    weights = [(1 << 20) // math.isqrt(rank ** skew) + 1 for rank in range(1, count + 1)]
    largest = limit if full else min(limit, max(-(-total // count), total * weights[0] // sum(weights)))
    least = 1 if total - largest >= count - 1 else 0
    holding, spare = [largest] + [least] * (count - 1), total - largest - least * (count - 1)
    while spare > 0:
        candidates = [i for i in range(1, count) if holding[i] < largest] or [i for i in range(1, count) if holding[i] < limit]
        whole, remaining = sum([weights[i] for i in candidates]), spare
        for i in candidates:
            addition = min(limit - holding[i], max(1, remaining * weights[i] // whole), spare)
            holding[i] = holding[i] + addition
            spare = spare - addition
    return np.array(holding)


def bell_draw(stream_key, shape, scale, limit, split=(), kind=jnp.bfloat16):
    array = scale * jax.random.normal(stream_key, shape, jnp.float32)
    if split:
        array = array * steps_of(stream_key, shape, split, -0.22, 0.18)
    return jnp.clip(array, -limit, limit).astype(kind)


def setup_inputs(seed: int = 0, part: int = 0) -> dict:
    seeds = jax.random.split(jax.random.key(seed), 8)
    own_keys = jax.random.split(jax.random.fold_in(seeds[7], part), 8)
    tokens = bell_draw(own_keys[0], (TOKEN_ROWS, MODEL_WIDTH), 1.0, 6.0, ((0, 8), (1, 2)))
    output_gradient = bell_draw(own_keys[1], (TOKEN_ROWS, VALUE_WIDTH), 1.0, 6.0, ((0, 8),))
    frozen_value_weight = bell_draw(seeds[2], (MODEL_WIDTH, VALUE_WIDTH), MODEL_WIDTH ** -0.5, 0.0625, ((0, 2), (1, 2)))
    adapter_down_weight = bell_draw(own_keys[3], (ADAPTER_JOBS, ADAPTER_RANK, MODEL_WIDTH), MODEL_WIDTH ** -0.5, 0.0625, ((0, 4), (2, 2)))
    adapter_up_weight = bell_draw(own_keys[4], (ADAPTER_JOBS, ADAPTER_RANK, VALUE_WIDTH), VALUE_WIDTH ** -0.5, 0.25, ((0, 4), (2, 2)))
    deal_keys = jax.random.split(jax.random.fold_in(own_keys[5], 1), TOKEN_ROWS // ROWS_DEV)
    deal_turns = jax.random.permutation(jax.random.fold_in(own_keys[5], 3), TOKEN_ROWS // ROWS_DEV)
    deal = jax.vmap(lambda own, number: assign_block(jax.random.fold_in(own_keys[5], 2), own, number, ROWS_DEV, N_DP, 1, MOST, 2))(deal_keys, deal_turns).reshape((TOKEN_ROWS, 1))
    row_local_job = touch_ends(jax.random.randint(own_keys[6], (TOKEN_ROWS,), 0, JOB_DEV), jax.random.fold_in(own_keys[6], 1), 0, JOB_DEV - 1).astype(jnp.int32)
    return dict(tokens=tokens, output_gradient=output_gradient, frozen_value_weight=frozen_value_weight, adapter_down_weight=adapter_down_weight, adapter_up_weight=adapter_up_weight, deal=deal, row_local_job=row_local_job)


ADAPTER_SCALE = 2.0


def reference(tokens, output_gradient, frozen_value_weight, adapter_down_weight, adapter_up_weight, deal, row_local_job):
    row_job = (deal[:, 0] * JOB_DEV + row_local_job).astype(jnp.int32)
    frozen_output = jnp.dot(tokens, frozen_value_weight, preferred_element_type=jnp.float32)
    frozen_gradient = jnp.dot(output_gradient, frozen_value_weight.T, preferred_element_type=jnp.float32)
    block_count = TOKEN_ROWS // ROWS_DEV
    token_blocks = tokens.reshape(block_count, ROWS_DEV, MODEL_WIDTH)
    grad_blocks = output_gradient.reshape(block_count, ROWS_DEV, VALUE_WIDTH)
    job_blocks = row_job.reshape(block_count, ROWS_DEV)

    def one_block(summed_totals, block_item):
        down_gradient_sum, up_gradient_sum = summed_totals
        block_tokens, block_grads, jobs_per_block = block_item
        picked_down_weight = adapter_down_weight[jobs_per_block].astype(jnp.float32)
        picked_up_weight = adapter_up_weight[jobs_per_block].astype(jnp.float32)
        tokens_wide = block_tokens.astype(jnp.float32)
        grads_wide = block_grads.astype(jnp.float32)
        low_rank = jnp.einsum("rkd,rd->rk", picked_down_weight, tokens_wide).astype(jnp.bfloat16)
        grad_rank = jnp.einsum("rkv,rv->rk", picked_up_weight, grads_wide).astype(jnp.bfloat16)
        wide_rank_rows = low_rank.astype(jnp.float32)
        wide_gradient = grad_rank.astype(jnp.float32)
        adapter_output = (ADAPTER_SCALE * jnp.einsum("ye,yez->yz", wide_rank_rows, picked_up_weight)).astype(jnp.bfloat16)
        adapter_gradient = (ADAPTER_SCALE * jnp.einsum("we,wep->wp", wide_gradient, picked_down_weight)).astype(jnp.bfloat16)
        term_down = wide_gradient[:, :, None] * tokens_wide[:, None, :]
        term_up = wide_rank_rows[:, :, None] * grads_wide[:, None, :]
        down_gradient_sum = down_gradient_sum + jax.ops.segment_sum(term_down, jobs_per_block, num_segments=ADAPTER_JOBS)
        up_gradient_sum = up_gradient_sum + jax.ops.segment_sum(term_up, jobs_per_block, num_segments=ADAPTER_JOBS)
        return (down_gradient_sum, up_gradient_sum), (adapter_output, adapter_gradient)

    start_totals = (jnp.zeros((ADAPTER_JOBS, ADAPTER_RANK, MODEL_WIDTH), jnp.float32), jnp.zeros((ADAPTER_JOBS, ADAPTER_RANK, VALUE_WIDTH), jnp.float32))
    summed_totals, result_list = lax.scan(one_block, start_totals, (token_blocks, grad_blocks, job_blocks))
    adapter_output = result_list[0].reshape(TOKEN_ROWS, VALUE_WIDTH)
    adapter_gradient = result_list[1].reshape(TOKEN_ROWS, MODEL_WIDTH)
    value_output = (frozen_output + adapter_output.astype(jnp.float32)).astype(jnp.bfloat16)
    input_gradient = (frozen_gradient + adapter_gradient.astype(jnp.float32)).astype(jnp.bfloat16)
    down_weight_gradient = ADAPTER_SCALE * summed_totals[0]
    up_weight_gradient = ADAPTER_SCALE * summed_totals[1]
    return value_output, input_gradient, down_weight_gradient, up_weight_gradient
```

```python
import jax
import jax.numpy as jnp
from jax import lax
from jax.sharding import PartitionSpec as P

ADAPTER_SCALE = 2.0


CONTRACT_LAST = (((1,), (1,)), ((), ()))
CONTRACT_FIRST = (((0,), (0,)), ((), ()))


def swap(extent, flip=1):
    return [(i, i ^ flip) for i in range(extent)]


def dot(left, right, dims=(((1,), (0,)), ((), ()))):
    return lax.dot_general(left, right, dims, preferred_element_type=jnp.float32)


def gather_adapters(
    tokens,
    output_gradient,
    frozen_value_weight,
    adapter_down_weight,
    adapter_up_weight,
    deal,
    row_local_job,
):
    rows, width_half = tokens.shape
    jobs, rank, features = adapter_up_weight.shape
    span = jobs * rank
    rep_index, dp_index = lax.axis_index("rep"), lax.axis_index("dp")
    fsdp_index, tp_index = lax.axis_index("fsdp"), lax.axis_index("tp")
    down = adapter_down_weight.reshape(span, width_half)
    up = adapter_up_weight.reshape(span, features)
    up_pair = jnp.stack([up, lax.ppermute(up, "tp", swap(2))])
    ups = [up_pair] + [lax.ppermute(up_pair, "dp", swap(4, k)) for k in (1, 2, 3)]
    outward = [(1, 0), (2, 3)]
    middle = [(1, 2), (2, 1)]
    down_next = lax.ppermute(down, "dp", swap(4))
    down_cross = lax.ppermute(down, "dp", middle)
    down_cross2 = lax.ppermute(down_next, "dp", middle)
    down_out = lax.ppermute(down_cross, "dp", outward)
    down_out2 = lax.ppermute(down_cross2, "dp", outward)
    downs = [down, down_next, down_cross + down_out, down_cross2 + down_out2]
    mid_index = jnp.where(dp_index < 2, 2, 1)
    end_index = jnp.where(dp_index < 2, 3, 0)
    holders = [dp_index, dp_index ^ 1, mid_index, end_index]
    weight_half = width_half // 2
    piece = weight_half // 2
    sent_half = lax.dynamic_slice_in_dim(frozen_value_weight, rep_index * weight_half, weight_half, 0)
    deal_row = deal.reshape(1, rows)
    job_row = row_local_job.reshape(1, rows)
    job_mask = (jnp.arange(span, dtype=jnp.int32) // rank)[:, None] == job_row
    grad_mine = lax.dynamic_slice_in_dim(output_gradient, tp_index * features, features, 1)
    grad_other = lax.dynamic_slice_in_dim(output_gradient, (1 - tp_index) * features, features, 1)
    grad_sum = jnp.zeros((span, rows), jnp.float32)
    for k in range(4):
        every = dot(ups[k][0], grad_mine, CONTRACT_LAST) + dot(ups[k][1], grad_other, CONTRACT_LAST)
        grad_sum = grad_sum + jnp.where(deal_row == (dp_index ^ k), every, 0)
    grad_rank = jnp.where(job_mask, grad_sum, 0).astype(jnp.bfloat16)
    zero = jnp.zeros((), jnp.bfloat16)

    def wide_of(narrow, k):
        return jnp.where(deal_row == holders[k], narrow, zero)

    halves = grad_rank.reshape(jobs, 2, rank // 2, rows)
    kept = lax.dynamic_index_in_dim(halves, fsdp_index, 1, False).reshape(span // 2, rows)
    sent = lax.dynamic_index_in_dim(halves, 1 - fsdp_index, 1, False).reshape(span // 2, rows)

    def down_part(narrow, ks):
        wide = jnp.concatenate([wide_of(narrow, k) for k in ks])
        return ADAPTER_SCALE * dot(wide, tokens)

    send_far = down_part(sent, (3, 2)).astype(jnp.bfloat16)
    send_near = down_part(sent, (1, 0)).astype(jnp.bfloat16)
    keep_far = down_part(kept, (3, 2))
    keep_near = down_part(kept, (1, 0))
    got_first = lax.ppermute(sent_half[:piece], "fsdp", swap(2))
    got_far = lax.ppermute(send_far, "fsdp", swap(2))
    got_near = lax.ppermute(send_near, "fsdp", swap(2))
    second, _ = lax.optimization_barrier((sent_half[piece:], send_near))
    got_second = lax.ppermute(second, "fsdp", swap(2))
    relay_first = lax.ppermute(got_first, "rep", swap(2))
    relay_second = lax.ppermute(got_second, "rep", swap(2))
    far = (keep_far + got_far.astype(jnp.float32)).astype(jnp.bfloat16)
    near = keep_near + got_near.astype(jnp.float32)
    s2 = span // 2
    inward = [(0, 1), (3, 2)]
    in_end = lax.ppermute(far[:s2], "dp", inward)
    in_mid = lax.ppermute(far[s2:], "dp", inward)
    cross_end = lax.ppermute(far[:s2] + in_end, "dp", middle)
    cross_mid = lax.ppermute(far[s2:] + in_mid, "dp", middle)
    near_next = (near[:s2] + cross_end.astype(jnp.float32)).astype(jnp.bfloat16)
    last = lax.ppermute(near_next, "dp", swap(4))
    down_share = near[s2:] + cross_mid.astype(jnp.float32) + last.astype(jnp.float32)
    down_share = down_share.reshape(jobs, rank // 2, width_half)
    low_part = jnp.zeros((span, rows), jnp.float32)
    for k in range(4):
        low_part = low_part + jnp.where(deal_row == holders[k], dot(downs[k], tokens, CONTRACT_LAST), 0)
    low_part = jnp.where(job_mask, low_part, 0)
    low_rank = (low_part + lax.ppermute(low_part, "tp", swap(2))).astype(jnp.bfloat16)
    wide_low = jnp.concatenate([jnp.where(deal_row == s, low_rank, zero) for s in range(4)])
    up_part = (ADAPTER_SCALE * dot(wide_low, grad_mine)).astype(jnp.bfloat16)
    up_part = up_part.reshape(4, jobs, 2, rank // 2, features).transpose(0, 2, 1, 3, 4)
    up_part = up_part.reshape(8, jobs * rank // 2, features)
    up_got = lax.all_to_all(up_part, ("dp", "fsdp"), split_axis=0, concat_axis=0, tiled=True)
    up_share = jnp.sum(up_got.astype(jnp.float32), axis=0).reshape(jobs, rank // 2, features)
    adapter_output = sum(
        dot(jnp.where(deal_row == (dp_index ^ k), low_rank, zero), ups[k][0], CONTRACT_FIRST) for k in range(4)
    )
    direct = jnp.concatenate([got_first, got_second])
    relayed = jnp.concatenate([relay_first, relay_second])
    low_half = jnp.where(rep_index == 0, direct, relayed)
    high_half = jnp.where(rep_index == 0, relayed, direct)
    other_weight = jnp.concatenate([low_half, high_half])
    own_out = dot(tokens, frozen_value_weight)
    other_out = dot(tokens, other_weight)
    same = fsdp_index == tp_index
    base_keep = jnp.where(same, own_out, other_out)
    base_send = jnp.where(same, other_out, own_out)
    base_out = base_keep + lax.ppermute(base_send, "tp", swap(2))
    value_output = (base_out + ADAPTER_SCALE * adapter_output).astype(jnp.bfloat16)
    grad_own = jnp.where(same, grad_mine, grad_other)
    grad_far = jnp.where(same, grad_other, grad_mine)
    lora = sum(dot(wide_of(grad_rank, k), downs[k], CONTRACT_FIRST) for k in range(4))
    input_gradient = dot(grad_own, frozen_value_weight, CONTRACT_LAST)
    input_gradient = input_gradient + dot(grad_far, other_weight, CONTRACT_LAST) + ADAPTER_SCALE * lora
    return value_output, input_gradient.astype(jnp.bfloat16), down_share, up_share


def dispatch_rows(
    tokens,
    output_gradient,
    frozen_value_weight,
    adapter_down_weight,
    adapter_up_weight,
    deal,
    row_local_job,
):
    row_count = tokens.shape[0]
    width_half = tokens.shape[1]
    jobs_owned_here = adapter_down_weight.shape[0]
    rank_extent = adapter_down_weight.shape[1]
    partial_value_rows = adapter_up_weight.shape[2]
    partner_count = lax.axis_size("dp")
    job_slot_count = 5 * row_count // (4 * partner_count)
    slot_total = partner_count * job_slot_count
    tp_index = lax.axis_index("tp")
    grad_part = lax.dynamic_slice_in_dim(
        output_gradient, tp_index * partial_value_rows, partial_value_rows, 1
    )
    contract_last = (((1,), (1,)), ((), ()))
    full_weight = lax.all_gather(frozen_value_weight, "fsdp", axis=1, tiled=True)
    frozen_output = jnp.dot(tokens, full_weight, preferred_element_type=jnp.float32)
    frozen_gradient = lax.dot_general(
        output_gradient, full_weight, contract_last, preferred_element_type=jnp.float32
    )
    value_share = lax.psum_scatter(frozen_output, "tp", scatter_dimension=1, tiled=True)
    row_dest = deal[:, 0]
    dest_onehot = (row_dest[:, None] == jnp.arange(partner_count, dtype=jnp.int32)[None, :]).astype(
        jnp.int32
    )
    earlier = jnp.cumsum(dest_onehot, axis=0) - dest_onehot
    slot_rank = jnp.sum(earlier * dest_onehot, axis=1)
    row_slot = row_dest * job_slot_count + slot_rank
    row_ids = jnp.arange(row_count, dtype=jnp.int32)
    slot_full = jnp.zeros((slot_total,), jnp.int32).at[row_slot].set(1)
    source_row = jnp.zeros((slot_total,), jnp.int32).at[row_slot].set(row_ids)
    is_full = slot_full > 0
    send_tokens = jnp.where(is_full[:, None], tokens[source_row], jnp.zeros((), jnp.bfloat16))
    send_grads = jnp.where(is_full[:, None], grad_part[source_row], jnp.zeros((), jnp.bfloat16))
    send_jobs = jnp.where(is_full, row_local_job[source_row], -1)
    got_tokens, got_grads, got_jobs = (
        lax.all_to_all(
            send_tokens.reshape(partner_count, job_slot_count, width_half),
            "dp",
            split_axis=0,
            concat_axis=0,
            tiled=True,
        ),
        lax.all_to_all(
            send_grads.reshape(partner_count, job_slot_count, partial_value_rows),
            "dp",
            split_axis=0,
            concat_axis=0,
            tiled=True,
        ),
        lax.all_to_all(
            send_jobs.reshape(partner_count, job_slot_count),
            "dp",
            split_axis=0,
            concat_axis=0,
            tiled=True,
        ),
    )
    got_tokens = got_tokens.reshape(slot_total, width_half)
    got_grads = got_grads.reshape(slot_total, partial_value_rows)
    got_jobs = got_jobs.reshape(slot_total)
    job_pick = got_jobs[:, None] == jnp.arange(jobs_owned_here, dtype=jnp.int32)[None, :]
    flat_down_weight = adapter_down_weight.reshape(jobs_owned_here * rank_extent, width_half)
    flat_up_weight = adapter_up_weight.reshape(jobs_owned_here * rank_extent, partial_value_rows)
    every_down = lax.dot_general(
        got_tokens, flat_down_weight, contract_last, preferred_element_type=jnp.float32
    )
    every_up = lax.dot_general(
        got_grads, flat_up_weight, contract_last, preferred_element_type=jnp.float32
    )
    pick_mask = job_pick.astype(jnp.float32)[:, :, None]
    low_partial = jnp.sum(
        every_down.reshape(slot_total, jobs_owned_here, rank_extent) * pick_mask, axis=1
    )
    grad_partial = jnp.sum(
        every_up.reshape(slot_total, jobs_owned_here, rank_extent) * pick_mask, axis=1
    )
    low_rank, grad_rank = lax.psum((low_partial, grad_partial), "tp")
    pick_narrow = job_pick.astype(jnp.bfloat16)[:, :, None]
    wide_rank_rows = (pick_narrow * low_rank.astype(jnp.bfloat16)[:, None, :]).reshape(
        slot_total, jobs_owned_here * rank_extent
    )
    wide_gradient = (pick_narrow * grad_rank.astype(jnp.bfloat16)[:, None, :]).reshape(
        slot_total, jobs_owned_here * rank_extent
    )
    adapter_output = (
        ADAPTER_SCALE * jnp.dot(wide_rank_rows, flat_up_weight, preferred_element_type=jnp.float32)
    ).astype(jnp.bfloat16)
    adapter_gradient = (
        ADAPTER_SCALE * jnp.dot(wide_gradient, flat_down_weight, preferred_element_type=jnp.float32)
    ).astype(jnp.bfloat16)
    contract_first = (((0,), (0,)), ((), ()))
    down_product = ADAPTER_SCALE * lax.dot_general(
        wide_gradient, got_tokens, contract_first, preferred_element_type=jnp.float32
    )
    up_product = ADAPTER_SCALE * lax.dot_general(
        wide_rank_rows, got_grads, contract_first, preferred_element_type=jnp.float32
    )
    down_share, up_share = (
        lax.psum_scatter(
            down_product.reshape(jobs_owned_here, rank_extent, width_half),
            "fsdp",
            scatter_dimension=1,
            tiled=True,
        ),
        lax.psum_scatter(
            up_product.reshape(jobs_owned_here, rank_extent, partial_value_rows),
            "fsdp",
            scatter_dimension=1,
            tiled=True,
        ),
    )
    back_out, back_grad = (
        lax.all_to_all(
            adapter_output.reshape(partner_count, job_slot_count, partial_value_rows),
            "dp",
            split_axis=0,
            concat_axis=0,
            tiled=True,
        ),
        lax.all_to_all(
            adapter_gradient.reshape(partner_count, job_slot_count, width_half),
            "dp",
            split_axis=0,
            concat_axis=0,
            tiled=True,
        ),
    )
    row_out = back_out.reshape(slot_total, partial_value_rows)[row_slot]
    row_grad = back_grad.reshape(slot_total, width_half)[row_slot]
    value_output = (value_share + row_out.astype(jnp.float32)).astype(jnp.bfloat16)
    input_gradient = (frozen_gradient + row_grad.astype(jnp.float32)).astype(jnp.bfloat16)
    return (value_output, input_gradient, down_share, up_share)


def solution(mesh):
    small = dict(mesh.shape) == {"rep": 2, "dp": 4, "fsdp": 2, "tp": 2}
    local = gather_adapters if small else dispatch_rows
    in_specs = (
        P(("rep", "dp", "fsdp"), "tp"),
        P(("rep", "dp", "fsdp"), None),
        P("tp", "fsdp"),
        P(("rep", "dp"), None, "tp"),
        P(("rep", "dp"), None, "tp"),
        P(("rep", "dp", "fsdp"), None),
        P(("rep", "dp", "fsdp")),
    )
    out_specs = (
        P(("rep", "dp", "fsdp"), "tp"),
        P(("rep", "dp", "fsdp"), "tp"),
        P(("rep", "dp"), "fsdp", "tp"),
        P(("rep", "dp"), "fsdp", "tp"),
    )
    return jax.shard_map(local, mesh=mesh, in_specs=in_specs, out_specs=out_specs, check_vma=False)
```

```python
import functools

import jax
import jax.numpy as jnp
from jax import lax
from jax.experimental import pallas as pl
from jax.experimental.pallas import tpu as pltpu
from jax.sharding import PartitionSpec as P

ADAPTER_SCALE = 2.0

BF16 = jnp.bfloat16
F32 = jnp.float32
PLAIN = (((1,), (0,)), ((), ()))
CONTRACT_LAST = (((1,), (1,)), ((), ()))
VMEM_BYTES = 16 * 1024 * 1024
COLUMNS = 1024
PART_US = 2
SEND_US = 6
FAR_US = 6
SUM_US = 6
NEAR_US = 6
UP_US = 4
LAST_US = 8
FIRST_SHARE = 4
WHOLE = pl.BlockSpec(memory_space=pltpu.VMEM)
ANY = pl.BlockSpec(memory_space=pl.ANY)
HBM = pl.BlockSpec(memory_space=pltpu.HBM)


def swap(extent, flip=1):
    return [(i, i ^ flip) for i in range(extent)]


def dot(left, right, dims=PLAIN):
    return lax.dot_general(left, right, dims, preferred_element_type=F32)


def struct(shape, dtype):
    return jax.ShapeDtypeStruct(shape, dtype)


def holders():
    here = lax.axis_index("dp")
    return here, here ^ 1, jnp.where(here < 2, 2, 1), jnp.where(here < 2, 3, 0)


def job_mask(span, rank, job_row):
    return lax.broadcasted_iota(jnp.int32, (span, job_row.shape[1]), 0) // rank == job_row


def prepare_kernel(gradient, deal, job, up, part_out, deal_out, job_out, up_out):
    features = up.shape[1]
    start = pl.multiple_of(lax.axis_index("tp") * features, features)
    part_out[...] = gradient[:, pl.ds(start, features)]
    deal_out[...] = deal[...]
    job_out[...] = job[...]
    up_out[...] = up[...]


def grad_partial_kernel(rank, near, far, gradient, deal, job, out):
    here = lax.axis_index("dp")
    span = out.shape[0]
    part = gradient[...]
    owner = deal[...]
    total = jnp.zeros(out.shape, F32)
    for k in range(4):
        block = (near, far)[k // 2][k % 2 * span : (k % 2 + 1) * span]
        total += jnp.where(owner == (here ^ k), dot(block, part, CONTRACT_LAST), 0.0)
    out[...] = jnp.where(job_mask(span, rank, job[...]), total, 0.0)


def each_column(ref):
    def run(body):
        def step(i, carry):
            body(pl.ds(pl.multiple_of(i * COLUMNS, COLUMNS), COLUMNS))
            return carry

        lax.fori_loop(0, ref.shape[1] // COLUMNS, step, 0)

    return run


def half_rows(narrow, rank, which):
    half = rank // 2
    pick = [narrow[j * half : (j + 1) * half] for j in range(narrow.shape[0] // half)]
    low, high = jnp.concatenate(pick[0::2]), jnp.concatenate(pick[1::2])
    return jnp.where(which == 0, low, high)


def wide_rows(narrow, owner, names):
    return jnp.concatenate([jnp.where(owner == name, narrow, 0.0) for name in names]).astype(BF16)


def grad_send_kernel(rank, first, second, deal, tokens, rank_out, far_out, near_out):
    total = first[...] + second[...]
    rank_out[...] = total.astype(BF16)
    total = total.astype(BF16).astype(F32)
    sent = ADAPTER_SCALE * half_rows(total, rank, 1 - lax.axis_index("fsdp"))
    mine, beside, middle, end = holders()
    wide = wide_rows(sent, deal[...], (end, middle, beside, mine))
    split = far_out.shape[0]

    @each_column(tokens)
    def _(at):
        made = dot(wide, tokens[:, at])
        far_out[:, at] = made[:split].astype(BF16)
        near_out[:, at] = made[split:].astype(BF16)


def kept_rows(rank, grad_rank):
    return ADAPTER_SCALE * half_rows(grad_rank[...].astype(F32), rank, lax.axis_index("fsdp"))


def in_middle():
    here = lax.axis_index("dp")
    return (here == 1) | (here == 2)


def far_kernel(rank, got, grad_rank, deal, tokens, down_cross, out, swap_out):
    _, _, middle, end = holders()
    wide = wide_rows(kept_rows(rank, grad_rank), deal[...], (end, middle))

    @each_column(tokens)
    def _(at):
        made = (dot(wide, tokens[:, at]) + got[:, at].astype(F32)).astype(BF16)
        out[:, at] = made
        swap_out[:, at] = jnp.where(in_middle(), down_cross[:, at], made)


def near_kernel(rank, got, grad_rank, deal, tokens, cross, next_out, mine_out):
    mine, beside, _, _ = holders()
    wide = wide_rows(kept_rows(rank, grad_rank), deal[...], (beside, mine))
    split = next_out.shape[0]

    @each_column(tokens)
    def _(at):
        made = dot(wide, tokens[:, at]) + got[:, at].astype(F32) + cross[:, at].astype(F32)
        next_out[:, at] = made[:split].astype(BF16)
        mine_out[:, at] = made[split:]


def low_kernel(rank, names, blocks, *refs):
    tokens, deal, job = refs[:3]
    out = refs[-1]
    owner = deal[...]
    name = holders()
    started = len(refs) - 4 > sum(blocks)
    out[...] = jnp.zeros(out.shape, F32)

    @each_column(tokens)
    def _(at):
        left = list(refs[3:-1])
        total = out[...]
        for k, count in zip(names, blocks):
            block = left.pop(0)[:, at]
            if count == 2:
                block = jnp.where(in_middle(), block, left.pop(0)[:, at])
            total += jnp.where(owner == name[k], dot(block, tokens[:, at], CONTRACT_LAST), 0.0)
        out[...] = total

    out[...] = jnp.where(job_mask(out.shape[0], rank, job[...]), out[...], 0.0)
    if started:
        out[...] += refs[-2][...]


def up_kernel(rank, low, low_got, gradient, deal, near, far, keep_out, away_out, lora_out):
    here = lax.axis_index("dp")
    span = low.shape[0]
    half = span // 2
    narrow = (low[...] + low_got[...]).astype(BF16).astype(F32)
    owner = deal[...]
    part = gradient[...]
    wide = jnp.concatenate([jnp.where(owner == (here ^ k), narrow, 0.0) for k in range(4)])
    made = ADAPTER_SCALE * dot(wide.astype(BF16), part)
    side = lax.axis_index("fsdp")
    for k in range(4):
        block = made[k * span : (k + 1) * span]
        keep_out[k * half : (k + 1) * half] = half_rows(block, rank, side)
        away_out[k * half : (k + 1) * half] = half_rows(block, rank, 1 - side).astype(BF16)
    ups = jnp.concatenate([near[...], far[...]])
    lora_out[...] = ADAPTER_SCALE * dot(wide.T.astype(BF16), ups)


def up_sum_kernel(keep, got, mine, *sent):
    total = keep[...] + got[...].astype(F32)
    half = mine.shape[0]
    mine[...] = total[:half]
    for k, out in enumerate(sent):
        out[...] = total[(k + 1) * half : (k + 2) * half].astype(BF16)


def own_kernel(tokens, own, out):
    out[...] = dot(tokens[...], own[...])


def base_kernel(offset, gradient, grad_rank, deal, direct, relayed, tokens, own, *refs):
    downs, (grad_out, other_out) = refs[:6], refs[-10:-8]
    wide, buffer, weight_in, own_in, token_in, down_in, sems, out_sems = refs[-8:]
    features = own.shape[1]
    count = direct.shape[0]
    mine = pl.multiple_of(lax.axis_index("fsdp") * features, features)
    other = pl.multiple_of((1 - lax.axis_index("fsdp")) * features, features)
    rep = lax.axis_index("rep")
    spots = []
    for side in range(2):
        start = (rep ^ side) * (own.shape[0] // 2) + offset
        spots.append(pl.ds(pl.multiple_of(start, 256), count))
    copies = []
    for side, (at, weight) in enumerate(zip(spots, (direct, relayed))):
        wanted = [(own.at[at, :], own_in.at[side]), (weight, weight_in.at[side])]
        wanted += [(down.at[:, at], down_in.at[side, k]) for k, down in enumerate(downs)]
        wanted += [(tokens.at[:, at], token_in.at[side])]
        copies.append([pltpu.make_async_copy(*pair, sems.at[side, i]) for i, pair in enumerate(wanted)])
        for copy in copies[-1]:
            copy.start()
    narrow = ADAPTER_SCALE * grad_rank[...].astype(F32)
    wide[...] = jnp.concatenate([jnp.where(deal[...] == name, narrow, 0.0) for name in holders()]).T.astype(BF16)
    stores = []
    for side, at in enumerate(spots):
        for copy in copies[side][:-1]:
            copy.wait()
        total = dot(gradient[:, pl.ds(mine, features)], own_in[side], CONTRACT_LAST)
        total += dot(gradient[:, pl.ds(other, features)], weight_in[side], CONTRACT_LAST)
        parts = [down_in[side, k] for k in range(6)]
        parts[2:] = [jnp.where(in_middle(), parts[k], parts[k + 1]) for k in (2, 4)]
        total += dot(wide[...], jnp.concatenate(parts))
        buffer[side] = total.astype(BF16)
        stores.append(pltpu.make_async_copy(buffer.at[side], grad_out.at[:, at], out_sems.at[side]))
        stores[-1].start()
        copies[side][-1].wait()
        other_part = dot(token_in[side], weight_in[side])
        other_out[...] = other_part if side == 0 else other_out[...] + other_part
    for store in stores:
        store.wait()


def call(kernel, out_shape, *args, after=(), in_specs=None, out_specs=None, us=0, **more):
    count = len(args)
    if out_specs is None:
        out_specs = (WHOLE,) * len(out_shape) if isinstance(out_shape, tuple) else WHOLE
    if after:
        inner = kernel
        kernel = lambda *refs: inner(*refs[:count], *refs[count + len(after) :])
    return pl.pallas_call(
        kernel,
        out_shape=out_shape,
        in_specs=(in_specs or [WHOLE] * count) + [ANY] * len(after),
        out_specs=out_specs,
        compiler_params=pltpu.CompilerParams(vmem_limit_bytes=VMEM_BYTES),
        cost_estimate=pl.CostEstimate(flops=int(us * 1.15e9), bytes_accessed=0, transcendentals=0) if us else None,
        **more,
    )(*args, *after)


def cut_kernel(weight, first, second, sems):
    half = weight.shape[0] // 2
    start = pl.multiple_of(lax.axis_index("rep") * half, half)
    count = first.shape[0]
    copies = [
        pltpu.make_async_copy(weight.at[pl.ds(start, count)], first, sems.at[0]),
        pltpu.make_async_copy(weight.at[pl.ds(start + count, half - count)], second, sems.at[1]),
    ]
    for copy in copies:
        copy.start()
    for copy in copies:
        copy.wait()


def join_kernel(one, two, out):
    half = one.shape[0]
    out[:half] = one[...]
    out[half:] = two[...]


def share_kernel(own, first, second, lora, send_out, keep_out):
    other = first[...] + second[...]
    same = lax.axis_index("fsdp") == lax.axis_index("tp")
    send_out[...] = jnp.where(same, other, own[...])
    keep_out[...] = jnp.where(same, own[...], other) + lora[...]


def total_kernel(*refs):
    total = refs[0][...]
    for ref in refs[1:-1]:
        total += ref[...].astype(F32)
    refs[-1][...] = total.astype(refs[-1].dtype)


def add_kernel(one, two, out):
    out[...] = (one[...].astype(F32) + two[...].astype(F32)).astype(BF16)


def ordered(value, before):
    return lax.optimization_barrier((value, before))[0]


def gather_adapters(
    tokens,
    output_gradient,
    frozen_value_weight,
    adapter_down_weight,
    adapter_up_weight,
    deal,
    row_local_job,
):
    rows, width = tokens.shape
    jobs, rank, features = adapter_up_weight.shape
    span = jobs * rank
    half = span // 2
    down = adapter_down_weight.reshape(span, width)
    up = adapter_up_weight.reshape(span, features)
    deal = deal.reshape(1, rows)
    job = row_local_job.reshape(1, rows)
    first_rows = width * FIRST_SHARE // 16
    outward, middle = [(1, 0), (2, 3)], [(1, 2), (2, 1)]

    up_got_first = lax.ppermute(up, "dp", swap(4))
    row = struct((1, rows), jnp.int32)
    grad_mine, deal, job, up = call(
        prepare_kernel, (struct((rows, features), BF16), row, row, struct((span, features), BF16)),
        output_gradient, deal, job, up,
    )
    up_pair = call(join_kernel, struct((2 * span, features), BF16), up, up_got_first, after=(grad_mine,))
    ups = up_pair, lax.ppermute(up_pair, "dp", swap(4, 2))
    weight_first, weight_second = call(
        cut_kernel,
        (struct((first_rows, features), BF16), struct((width // 2 - first_rows, features), BF16)),
        frozen_value_weight,
        in_specs=[ANY],
        out_specs=(ANY, ANY),
        scratch_shapes=[pltpu.SemaphoreType.DMA((2,))],
    )
    got_first = lax.ppermute(weight_first, "fsdp", swap(2))

    narrow = struct((span, rows), F32)
    half_wide = struct((half, width), BF16)
    span_wide = struct((span, width), BF16)
    grad_part = call(functools.partial(grad_partial_kernel, rank), narrow, *ups, grad_mine, deal, job, us=PART_US)
    grad_got = lax.ppermute(grad_part, "tp", swap(2))
    grad_rank, send_far, send_near = call(
        functools.partial(grad_send_kernel, rank), (struct((span, rows), BF16), span_wide, span_wide),
        grad_part, grad_got, deal, tokens, after=(got_first,), us=SEND_US,
    )
    down_sent = ordered(down, send_far)
    down_next = lax.ppermute(down_sent, "dp", swap(4))
    down_cross = lax.ppermute(down_sent, "dp", middle)
    got_far = lax.ppermute(send_far, "fsdp", swap(2))
    relay_first = lax.ppermute(ordered(got_first, send_far), "rep", swap(2))
    own_out = call(
        own_kernel, struct((rows, features), F32), tokens, frozen_value_weight, after=(send_far,)
    )
    far, far_swap = call(
        functools.partial(far_kernel, rank), (span_wide, span_wide),
        got_far, grad_rank, deal, tokens, down_cross, after=(own_out, relay_first), us=FAR_US,
    )
    got_second = lax.ppermute(ordered(weight_second, got_far), "fsdp", swap(2))
    swapped = lax.ppermute(far_swap, "dp", swap(4))
    down_cross2 = lax.ppermute(ordered(down_next, far), "dp", middle)
    low_near = call(
        functools.partial(low_kernel, rank, (0, 1), (1, 1)),
        narrow, tokens, deal, job, down, down_next, after=(far,),
    )
    low_first = call(
        functools.partial(low_kernel, rank, (2,), (2,)),
        narrow, tokens, deal, job, down_cross, swapped, low_near,
    )
    far_sum = call(add_kernel, span_wide, far, swapped, after=(got_second,), us=SUM_US)
    got_near = lax.ppermute(ordered(send_near, got_second), "fsdp", swap(2))
    cross = lax.ppermute(far_sum, "dp", middle)
    down_out2 = lax.ppermute(ordered(down_cross2, far_sum), "dp", outward)
    relay_second = lax.ppermute(got_second, "rep", swap(2))
    next_sum, mine_sum = call(
        functools.partial(near_kernel, rank), (half_wide, struct((half, width), F32)),
        got_near, grad_rank, deal, tokens, cross, us=NEAR_US,
    )
    last = lax.ppermute(next_sum, "dp", swap(4))
    low_part = call(
        functools.partial(low_kernel, rank, (3,), (2,)), narrow, tokens, deal, job, down_cross2, down_out2, low_first, after=(next_sum,)
    )
    low_got = lax.ppermute(low_part, "tp", swap(2))
    up_half = struct((4 * half, features), F32), struct((4 * half, features), BF16)
    up_keep, up_away, lora = call(
        functools.partial(up_kernel, rank), (*up_half, struct((rows, features), F32)),
        low_part, low_got, grad_mine, deal, *ups,
    )
    def base(offset, direct, relayed, *into):
        count = direct.shape[0]
        return call(
            functools.partial(base_kernel, offset),
            (struct((rows, width), BF16), struct((rows, features), F32)),
            output_gradient, grad_rank, deal, direct, relayed, tokens, frozen_value_weight,
            down, down_next, down_cross, swapped, down_cross2, down_out2,
            after=into,
            in_specs=[WHOLE] * 3 + [HBM] * 10,
            out_specs=(HBM, WHOLE),
            scratch_shapes=[
                pltpu.VMEM((rows, 4 * span), BF16),
                pltpu.VMEM((2, rows, count), BF16),
                pltpu.VMEM((2, count, features), BF16),
                pltpu.VMEM((2, count, features), BF16),
                pltpu.VMEM((2, rows, count), BF16),
                pltpu.VMEM((2, 6, span, count), BF16),
                pltpu.SemaphoreType.DMA((2, 9)),
                pltpu.SemaphoreType.DMA((2,)),
            ],
            input_output_aliases={13: 0} if into else {},
        )

    input_first, other_first = base(0, got_first, relay_first)
    up_got = lax.ppermute(up_away, "fsdp", swap(2))
    up_mine, *up_sent = call(
        up_sum_kernel, (struct((half, features), F32),) + (struct((half, features), BF16),) * 3, up_keep, up_got,
        us=UP_US,
    )
    up_last = [lax.ppermute(sent, "dp", swap(4, k + 1)) for k, sent in enumerate(up_sent)]
    up_share = call(total_kernel, struct((half, features), F32), up_mine, *up_last)

    input_gradient, other_second = base(first_rows, got_second, relay_second, input_first)
    base_send, base_keep = call(
        share_kernel, (struct((rows, features), F32),) * 2, own_out, other_first, other_second, lora
    )
    base_got = lax.ppermute(base_send, "tp", swap(2))
    value_output = call(total_kernel, struct((rows, features), BF16), base_keep, base_got)
    down_share = call(total_kernel, struct((half, width), F32), mine_sum, last, us=LAST_US)
    shares = [share.reshape(jobs, rank // 2, share.shape[1]) for share in (down_share, up_share)]
    return value_output, input_gradient, *shares


def dispatch_rows(
    tokens,
    output_gradient,
    frozen_value_weight,
    adapter_down_weight,
    adapter_up_weight,
    deal,
    row_local_job,
):
    row_count = tokens.shape[0]
    width_half = tokens.shape[1]
    jobs_owned_here = adapter_down_weight.shape[0]
    rank_extent = adapter_down_weight.shape[1]
    partial_value_rows = adapter_up_weight.shape[2]
    partner_count = lax.axis_size("dp")
    job_slot_count = 5 * row_count // (4 * partner_count)
    slot_total = partner_count * job_slot_count
    tp_index = lax.axis_index("tp")
    grad_part = lax.dynamic_slice_in_dim(
        output_gradient, tp_index * partial_value_rows, partial_value_rows, 1
    )
    contract_last = (((1,), (1,)), ((), ()))
    full_weight = lax.all_gather(frozen_value_weight, "fsdp", axis=1, tiled=True)
    frozen_output = jnp.dot(tokens, full_weight, preferred_element_type=jnp.float32)
    frozen_gradient = lax.dot_general(
        output_gradient, full_weight, contract_last, preferred_element_type=jnp.float32
    )
    value_share = lax.psum_scatter(frozen_output, "tp", scatter_dimension=1, tiled=True)
    row_dest = deal[:, 0]
    dest_onehot = (row_dest[:, None] == jnp.arange(partner_count, dtype=jnp.int32)[None, :]).astype(
        jnp.int32
    )
    earlier = jnp.cumsum(dest_onehot, axis=0) - dest_onehot
    slot_rank = jnp.sum(earlier * dest_onehot, axis=1)
    row_slot = row_dest * job_slot_count + slot_rank
    row_ids = jnp.arange(row_count, dtype=jnp.int32)
    slot_full = jnp.zeros((slot_total,), jnp.int32).at[row_slot].set(1)
    source_row = jnp.zeros((slot_total,), jnp.int32).at[row_slot].set(row_ids)
    is_full = slot_full > 0
    send_tokens = jnp.where(is_full[:, None], tokens[source_row], jnp.zeros((), jnp.bfloat16))
    send_grads = jnp.where(is_full[:, None], grad_part[source_row], jnp.zeros((), jnp.bfloat16))
    send_jobs = jnp.where(is_full, row_local_job[source_row], -1)
    got_tokens, got_grads, got_jobs = (
        lax.all_to_all(
            send_tokens.reshape(partner_count, job_slot_count, width_half),
            "dp",
            split_axis=0,
            concat_axis=0,
            tiled=True,
        ),
        lax.all_to_all(
            send_grads.reshape(partner_count, job_slot_count, partial_value_rows),
            "dp",
            split_axis=0,
            concat_axis=0,
            tiled=True,
        ),
        lax.all_to_all(
            send_jobs.reshape(partner_count, job_slot_count),
            "dp",
            split_axis=0,
            concat_axis=0,
            tiled=True,
        ),
    )
    got_tokens = got_tokens.reshape(slot_total, width_half)
    got_grads = got_grads.reshape(slot_total, partial_value_rows)
    got_jobs = got_jobs.reshape(slot_total)
    job_pick = got_jobs[:, None] == jnp.arange(jobs_owned_here, dtype=jnp.int32)[None, :]
    flat_down_weight = adapter_down_weight.reshape(jobs_owned_here * rank_extent, width_half)
    flat_up_weight = adapter_up_weight.reshape(jobs_owned_here * rank_extent, partial_value_rows)
    every_down = lax.dot_general(
        got_tokens, flat_down_weight, contract_last, preferred_element_type=jnp.float32
    )
    every_up = lax.dot_general(
        got_grads, flat_up_weight, contract_last, preferred_element_type=jnp.float32
    )
    pick_mask = job_pick.astype(jnp.float32)[:, :, None]
    low_partial = jnp.sum(
        every_down.reshape(slot_total, jobs_owned_here, rank_extent) * pick_mask, axis=1
    )
    grad_partial = jnp.sum(
        every_up.reshape(slot_total, jobs_owned_here, rank_extent) * pick_mask, axis=1
    )
    low_rank, grad_rank = lax.psum((low_partial, grad_partial), "tp")
    pick_narrow = job_pick.astype(jnp.bfloat16)[:, :, None]
    wide_rank_rows = (pick_narrow * low_rank.astype(jnp.bfloat16)[:, None, :]).reshape(
        slot_total, jobs_owned_here * rank_extent
    )
    wide_gradient = (pick_narrow * grad_rank.astype(jnp.bfloat16)[:, None, :]).reshape(
        slot_total, jobs_owned_here * rank_extent
    )
    adapter_output = (
        ADAPTER_SCALE * jnp.dot(wide_rank_rows, flat_up_weight, preferred_element_type=jnp.float32)
    ).astype(jnp.bfloat16)
    adapter_gradient = (
        ADAPTER_SCALE * jnp.dot(wide_gradient, flat_down_weight, preferred_element_type=jnp.float32)
    ).astype(jnp.bfloat16)
    contract_first = (((0,), (0,)), ((), ()))
    down_product = ADAPTER_SCALE * lax.dot_general(
        wide_gradient, got_tokens, contract_first, preferred_element_type=jnp.float32
    )
    up_product = ADAPTER_SCALE * lax.dot_general(
        wide_rank_rows, got_grads, contract_first, preferred_element_type=jnp.float32
    )
    down_share, up_share = (
        lax.psum_scatter(
            down_product.reshape(jobs_owned_here, rank_extent, width_half),
            "fsdp",
            scatter_dimension=1,
            tiled=True,
        ),
        lax.psum_scatter(
            up_product.reshape(jobs_owned_here, rank_extent, partial_value_rows),
            "fsdp",
            scatter_dimension=1,
            tiled=True,
        ),
    )
    back_out, back_grad = (
        lax.all_to_all(
            adapter_output.reshape(partner_count, job_slot_count, partial_value_rows),
            "dp",
            split_axis=0,
            concat_axis=0,
            tiled=True,
        ),
        lax.all_to_all(
            adapter_gradient.reshape(partner_count, job_slot_count, width_half),
            "dp",
            split_axis=0,
            concat_axis=0,
            tiled=True,
        ),
    )
    row_out = back_out.reshape(slot_total, partial_value_rows)[row_slot]
    row_grad = back_grad.reshape(slot_total, width_half)[row_slot]
    value_output = (value_share + row_out.astype(jnp.float32)).astype(jnp.bfloat16)
    input_gradient = (frozen_gradient + row_grad.astype(jnp.float32)).astype(jnp.bfloat16)
    return (value_output, input_gradient, down_share, up_share)


def solution(mesh):
    small = dict(mesh.shape) == {"rep": 2, "dp": 4, "fsdp": 2, "tp": 2}
    local = gather_adapters if small else dispatch_rows
    in_specs = (
        P(("rep", "dp", "fsdp"), "tp"),
        P(("rep", "dp", "fsdp"), None),
        P("tp", "fsdp"),
        P(("rep", "dp"), None, "tp"),
        P(("rep", "dp"), None, "tp"),
        P(("rep", "dp", "fsdp"), None),
        P(("rep", "dp", "fsdp")),
    )
    out_specs = (
        P(("rep", "dp", "fsdp"), "tp"),
        P(("rep", "dp", "fsdp"), "tp"),
        P(("rep", "dp"), "fsdp", "tp"),
        P(("rep", "dp"), "fsdp", "tp"),
    )
    return jax.shard_map(local, mesh=mesh, in_specs=in_specs, out_specs=out_specs, check_vma=False)
```

```python
import functools

import jax
import jax.numpy as jnp
from jax import lax
from jax.experimental import pallas as pl
from jax.experimental.pallas import tpu as pltpu
from jax.sharding import PartitionSpec as P

ADAPTER_SCALE = 2.0

BF16 = jnp.bfloat16
F32 = jnp.float32
PLAIN = (((1,), (0,)), ((), ()))
CONTRACT_LAST = (((1,), (1,)), ((), ()))
VMEM_BYTES = 10 * 1024 * 1024
COLUMNS = 1024
OWN_PARTS = 4
PART_US = 3.6
SEND_US = 6
FAR_US = 6
SUM_US = 6
NEAR_US = 6
UP_US = 4
LAST_US = 15
FIRST_SHARE = 4
WHOLE = pl.BlockSpec(memory_space=pltpu.VMEM)
ANY = pl.BlockSpec(memory_space=pl.ANY)
HBM = pl.BlockSpec(memory_space=pltpu.HBM)


def swap(extent, flip=1):
    return [(i, i ^ flip) for i in range(extent)]


def dot(left, right, dims=PLAIN):
    return lax.dot_general(left, right, dims, preferred_element_type=F32)


def struct(shape, dtype):
    return jax.ShapeDtypeStruct(shape, dtype)


def holders():
    here = lax.axis_index("dp")
    return here, here ^ 1, jnp.where(here < 2, 2, 1), jnp.where(here < 2, 3, 0)


def job_mask(span, rank, job_row):
    return lax.broadcasted_iota(jnp.int32, (span, job_row.shape[1]), 0) // rank == job_row


def prepare_kernel(gradient, deal, job, up, *refs):
    features = up.shape[1]
    start = pl.multiple_of(lax.axis_index("tp") * features, features)
    sources = gradient.at[:, pl.ds(start, features)], deal, job, up
    copies = [pltpu.make_async_copy(source, out, refs[4].at[k]) for k, (source, out) in enumerate(zip(sources, refs))]
    for copy in copies:
        copy.start()
    for copy in copies:
        copy.wait()


def grad_partial_kernel(rank, near, far, gradient, deal, job, out):
    here = lax.axis_index("dp")
    span = out.shape[0]
    part = gradient[...]
    owner = deal[...]
    total = jnp.zeros(out.shape, F32)
    for k in range(4):
        block = (near, far)[k // 2][k % 2 * span : (k % 2 + 1) * span]
        total += jnp.where(owner == (here ^ k), dot(block, part, CONTRACT_LAST), 0.0)
    out[...] = jnp.where(job_mask(span, rank, job[...]), total, 0.0)


def each_column(ref):
    def run(body):
        def step(i, carry):
            body(pl.ds(pl.multiple_of(i * COLUMNS, COLUMNS), COLUMNS))
            return carry

        lax.fori_loop(0, ref.shape[1] // COLUMNS, step, 0)

    return run


def half_rows(narrow, rank, which):
    half = rank // 2
    pick = [narrow[j * half : (j + 1) * half] for j in range(narrow.shape[0] // half)]
    low, high = jnp.concatenate(pick[0::2]), jnp.concatenate(pick[1::2])
    return jnp.where(which == 0, low, high)


def wide_rows(narrow, owner, names):
    return jnp.concatenate([jnp.where(owner == name, narrow, 0.0) for name in names]).astype(BF16)


def grad_send_kernel(rank, first, second, deal, tokens, rank_out, far_out, near_out):
    total = first[...] + second[...]
    rank_out[...] = total.astype(BF16)
    total = total.astype(BF16).astype(F32)
    sent = ADAPTER_SCALE * half_rows(total, rank, 1 - lax.axis_index("fsdp"))
    mine, beside, middle, end = holders()
    wide = wide_rows(sent, deal[...], (end, middle, beside, mine))
    split = far_out.shape[0]

    @each_column(tokens)
    def _(at):
        made = dot(wide, tokens[:, at])
        far_out[:, at] = made[:split].astype(BF16)
        near_out[:, at] = made[split:].astype(BF16)


def kept_rows(rank, grad_rank):
    return ADAPTER_SCALE * half_rows(grad_rank[...].astype(F32), rank, lax.axis_index("fsdp"))


def in_middle():
    here = lax.axis_index("dp")
    return (here == 1) | (here == 2)


def far_kernel(rank, got, grad_rank, deal, tokens, down_cross, out, swap_out):
    _, _, middle, end = holders()
    wide = wide_rows(kept_rows(rank, grad_rank), deal[...], (end, middle))

    @each_column(tokens)
    def _(at):
        made = (dot(wide, tokens[:, at]) + got[:, at].astype(F32)).astype(BF16)
        out[:, at] = made
        swap_out[:, at] = jnp.where(in_middle(), down_cross[:, at], made)


def near_kernel(rank, got, grad_rank, deal, cross, tokens, next_out, mine_out, held, sems):
    copies = [
        pltpu.make_async_copy(tokens.at[:, at], held.at[:, at], sems.at[k])
        for k, at in enumerate(pl.ds(k * COLUMNS, COLUMNS) for k in range(tokens.shape[1] // COLUMNS))
    ]
    for copy in copies:
        copy.start()
    mine, beside, _, _ = holders()
    wide = wide_rows(kept_rows(rank, grad_rank), deal[...], (beside, mine))
    split = next_out.shape[0]
    for k, copy in enumerate(copies):
        at = pl.ds(k * COLUMNS, COLUMNS)
        copy.wait()
        made = dot(wide, held[:, at]) + got[:, at].astype(F32) + cross[:, at].astype(F32)
        next_out[:, at] = made[:split].astype(BF16)
        mine_out[:, at] = made[split:]


def low_kernel(rank, names, blocks, *refs):
    tokens, deal, job = refs[:3]
    out = refs[-1]
    owner = deal[...]
    name = holders()
    started = len(refs) - 4 > sum(blocks)
    out[...] = jnp.zeros(out.shape, F32)

    @each_column(tokens)
    def _(at):
        left = list(refs[3:-1])
        total = out[...]
        for k, count in zip(names, blocks):
            block = left.pop(0)[:, at]
            if count == 2:
                block = jnp.where(in_middle(), block, left.pop(0)[:, at])
            total += jnp.where(owner == name[k], dot(block, tokens[:, at], CONTRACT_LAST), 0.0)
        out[...] = total

    out[...] = jnp.where(job_mask(out.shape[0], rank, job[...]), out[...], 0.0)
    if started:
        out[...] += refs[-2][...]


def up_kernel(rank, low, low_got, gradient, deal, near, far, keep_out, away_out, lora_out):
    here = lax.axis_index("dp")
    span = low.shape[0]
    half = span // 2
    narrow = (low[...] + low_got[...]).astype(BF16).astype(F32)
    owner = deal[...]
    part = gradient[...]
    wide = jnp.concatenate([jnp.where(owner == (here ^ k), narrow, 0.0) for k in range(4)])
    made = ADAPTER_SCALE * dot(wide.astype(BF16), part)
    side = lax.axis_index("fsdp")
    for k in range(4):
        block = made[k * span : (k + 1) * span]
        keep_out[k * half : (k + 1) * half] = half_rows(block, rank, side)
        away_out[k * half : (k + 1) * half] = half_rows(block, rank, 1 - side).astype(BF16)
    ups = jnp.concatenate([near[...], far[...]])
    lora_out[...] = ADAPTER_SCALE * dot(wide.T.astype(BF16), ups)


def up_sum_kernel(keep, got, mine, *sent):
    total = keep[...] + got[...].astype(F32)
    half = mine.shape[0]
    mine[...] = total[:half]
    for k, out in enumerate(sent):
        out[...] = total[(k + 1) * half : (k + 2) * half].astype(BF16)


def own_kernel(tokens, own, out, buffer, sems):
    count = own.shape[0] // OWN_PARTS
    copies = []
    for k in range(OWN_PARTS):
        at = pl.ds(k * count, count)
        copies.append(pltpu.make_async_copy(own.at[at], buffer.at[at], sems.at[k]))
        copies[-1].start()
    for k, copy in enumerate(copies):
        at = pl.ds(k * count, count)
        copy.wait()
        part = dot(tokens[:, at], buffer[at])
        out[...] = part if k == 0 else out[...] + part


def base_kernel(offset, gradient, grad_rank, deal, direct, relayed, *refs):
    downs, (tokens, own) = refs[:6], refs[6:8]
    grad_out, other_out, wide, buffer, own_in, token_in, sems, out_sems = refs[-8:]
    features = own.shape[1]
    count = direct.shape[0]
    mine = pl.multiple_of(lax.axis_index("fsdp") * features, features)
    other = pl.multiple_of((1 - lax.axis_index("fsdp")) * features, features)
    rep = lax.axis_index("rep")
    spots, copies, stores = [], [], []
    for side in range(2):
        start = (rep ^ side) * (own.shape[0] // 2) + offset
        spots.append(pl.ds(pl.multiple_of(start, 256), count))
        copies.append(
            [
                pltpu.make_async_copy(own.at[spots[side], :], own_in.at[side], sems.at[side, 0]),
                pltpu.make_async_copy(tokens.at[:, spots[side]], token_in.at[side], sems.at[side, 1]),
            ]
        )
        for copy in copies[side]:
            copy.start()
    narrow = ADAPTER_SCALE * grad_rank[...].astype(F32)
    wide[...] = jnp.concatenate([jnp.where(deal[...] == name, narrow, 0.0) for name in holders()]).T.astype(BF16)
    for side, (at, weight) in enumerate(zip(spots, (direct, relayed))):
        parts = [down[:, at] for down in downs]
        parts[2:] = [jnp.where(in_middle(), parts[k], parts[k + 1]) for k in (2, 4)]
        total = dot(wide[...], jnp.concatenate(parts))
        total += dot(gradient[:, pl.ds(other, features)], weight[...], CONTRACT_LAST)
        copies[side][0].wait()
        total += dot(gradient[:, pl.ds(mine, features)], own_in[side], CONTRACT_LAST)
        buffer[side] = total.astype(BF16)
        stores.append(pltpu.make_async_copy(buffer.at[side], grad_out.at[:, at], out_sems.at[side]))
        stores[side].start()
        copies[side][1].wait()
        other_part = dot(token_in[side], weight[...])
        other_out[...] = other_part if side == 0 else other_out[...] + other_part
    for store in stores:
        store.wait()


def call(kernel, out_shape, *args, after=(), in_specs=None, out_specs=None, us=0, **more):
    count = len(args)
    if out_specs is None:
        out_specs = (WHOLE,) * len(out_shape) if isinstance(out_shape, tuple) else WHOLE
    if after:
        inner = kernel
        kernel = lambda *refs: inner(*refs[:count], *refs[count + len(after) :])
    return pl.pallas_call(
        kernel,
        out_shape=out_shape,
        in_specs=(in_specs or [WHOLE] * count) + [ANY] * len(after),
        out_specs=out_specs,
        compiler_params=pltpu.CompilerParams(vmem_limit_bytes=VMEM_BYTES),
        cost_estimate=pl.CostEstimate(flops=int(us * 1.15e9), bytes_accessed=0, transcendentals=0) if us else None,
        **more,
    )(*args, *after)


def cut_kernel(weight, first, second, sems):
    half = weight.shape[0] // 2
    start = pl.multiple_of(lax.axis_index("rep") * half, half)
    count = first.shape[0]
    copies = [
        pltpu.make_async_copy(weight.at[pl.ds(start, count)], first, sems.at[0]),
        pltpu.make_async_copy(weight.at[pl.ds(start + count, half - count)], second, sems.at[1]),
    ]
    for copy in copies:
        copy.start()
    for copy in copies:
        copy.wait()


def join_kernel(one, two, out):
    half = one.shape[0]
    out[:half] = one[...]
    out[half:] = two[...]


def share_kernel(own, first, second, lora, send_out, keep_out):
    other = first[...] + second[...]
    same = lax.axis_index("fsdp") == lax.axis_index("tp")
    send_out[...] = jnp.where(same, other, own[...])
    keep_out[...] = jnp.where(same, own[...], other) + lora[...]


def total_kernel(*refs):
    total = refs[0][...]
    for ref in refs[1:-1]:
        total += ref[...].astype(F32)
    refs[-1][...] = total.astype(refs[-1].dtype)


def add_kernel(one, two, out):
    out[...] = (one[...].astype(F32) + two[...].astype(F32)).astype(BF16)


def ordered(value, before):
    return lax.optimization_barrier((value, before))[0]


def gather_adapters(
    tokens,
    output_gradient,
    frozen_value_weight,
    adapter_down_weight,
    adapter_up_weight,
    deal,
    row_local_job,
):
    rows, width = tokens.shape
    jobs, rank, features = adapter_up_weight.shape
    span = jobs * rank
    half = span // 2
    down = adapter_down_weight.reshape(span, width)
    up = adapter_up_weight.reshape(span, features)
    deal = deal.reshape(1, rows)
    job = row_local_job.reshape(1, rows)
    first_rows = width * FIRST_SHARE // 16
    outward, middle = [(1, 0), (2, 3)], [(1, 2), (2, 1)]

    up_got_first = lax.ppermute(up, "dp", swap(4))
    row = struct((1, rows), jnp.int32)
    grad_mine, deal, job, up = call(
        prepare_kernel, (struct((rows, features), BF16), row, row, struct((span, features), BF16)),
        output_gradient, deal, job, up,
        in_specs=[ANY] * 4, scratch_shapes=[pltpu.SemaphoreType.DMA((4,))],
    )
    up_pair = call(join_kernel, struct((2 * span, features), BF16), up, up_got_first, after=(grad_mine,))
    ups = up_pair, lax.ppermute(up_pair, "dp", swap(4, 2))
    weight_first, weight_second = call(
        cut_kernel,
        (struct((first_rows, features), BF16), struct((width // 2 - first_rows, features), BF16)),
        frozen_value_weight,
        in_specs=[HBM],
        out_specs=(ANY, ANY),
        scratch_shapes=[pltpu.SemaphoreType.DMA((2,))],
    )
    got_first = lax.ppermute(weight_first, "fsdp", swap(2))

    narrow = struct((span, rows), F32)
    half_wide = struct((half, width), BF16)
    span_wide = struct((span, width), BF16)
    grad_part = call(functools.partial(grad_partial_kernel, rank), narrow, *ups, grad_mine, deal, job, us=PART_US)
    grad_got = lax.ppermute(grad_part, "tp", swap(2))
    grad_rank, send_far, send_near = call(
        functools.partial(grad_send_kernel, rank), (struct((span, rows), BF16), span_wide, span_wide),
        grad_part, grad_got, deal, tokens, after=(got_first,), us=SEND_US,
    )
    down_sent = ordered(down, grad_part)
    down_next = lax.ppermute(down_sent, "dp", swap(4))
    down_cross = lax.ppermute(ordered(down, grad_part), "dp", middle)
    got_far = lax.ppermute(send_far, "fsdp", swap(2))
    own_out = call(
        own_kernel,
        struct((rows, features), F32),
        tokens,
        frozen_value_weight,
        after=(send_far,),
        in_specs=[WHOLE, HBM],
        scratch_shapes=[pltpu.VMEM((width, features), BF16), pltpu.SemaphoreType.DMA((OWN_PARTS,))],
    )
    relay_first = lax.ppermute(ordered(got_first, own_out), "rep", swap(2))
    far, far_swap = call(
        functools.partial(far_kernel, rank), (span_wide, span_wide),
        got_far, grad_rank, deal, tokens, down_cross, after=(own_out, down_next), us=FAR_US,
    )
    got_second = lax.ppermute(ordered(weight_second, got_far), "fsdp", swap(2))
    swapped = lax.ppermute(far_swap, "dp", swap(4))
    down_cross2 = lax.ppermute(ordered(down_next, down_cross), "dp", middle)
    low_near = call(
        functools.partial(low_kernel, rank, (0, 1), (1, 1)),
        narrow, tokens, deal, job, down, down_next, after=(far,),
    )
    low_first = call(
        functools.partial(low_kernel, rank, (2,), (2,)),
        narrow, tokens, deal, job, down_cross, swapped, low_near,
    )
    far_sum = call(add_kernel, span_wide, far, swapped, after=(got_second, down_cross2, relay_first, low_near), us=SUM_US)
    got_near = lax.ppermute(ordered(send_near, got_second), "fsdp", swap(2))
    cross = lax.ppermute(far_sum, "dp", middle)
    down_out2 = lax.ppermute(ordered(down_cross2, far), "dp", outward)
    relay_second = lax.ppermute(got_second, "rep", swap(2))
    low_part = call(
        functools.partial(low_kernel, rank, (3,), (2,)), narrow, tokens, deal, job, down_cross2, down_out2, low_first, after=()
    )
    low_got = lax.ppermute(low_part, "tp", swap(2))
    up_half = struct((4 * half, features), F32), struct((4 * half, features), BF16)
    up_keep, up_away, lora = call(
        functools.partial(up_kernel, rank), (*up_half, struct((rows, features), F32)),
        low_part, low_got, grad_mine, deal, *ups,
    )
    def base(offset, direct, relayed, *into):
        count = direct.shape[0]
        return call(
            functools.partial(base_kernel, offset),
            (struct((rows, width), BF16), struct((rows, features), F32)),
            output_gradient, grad_rank, deal, direct, relayed,
            down, down_next, down_cross, swapped, down_cross2, down_out2, tokens, frozen_value_weight,
            after=into,
            in_specs=[WHOLE] * 11 + [HBM] * 2,
            out_specs=(HBM, WHOLE),
            scratch_shapes=[
                pltpu.VMEM((rows, 4 * span), BF16),
                pltpu.VMEM((2, rows, count), BF16),
                pltpu.VMEM((2, count, features), BF16),
                pltpu.VMEM((2, rows, count), BF16),
                pltpu.SemaphoreType.DMA((2, 2)),
                pltpu.SemaphoreType.DMA((2,)),
            ],
            input_output_aliases={13: 0} if into else {},
        )

    input_first, other_first = base(0, got_first, relay_first)
    next_sum, mine_sum = call(
        functools.partial(near_kernel, rank), (half_wide, struct((half, width), F32)),
        got_near, grad_rank, deal, cross, tokens, after=(up_away, input_first, relay_second), us=NEAR_US,
        in_specs=[WHOLE] * 4 + [HBM],
        scratch_shapes=[pltpu.VMEM((rows, width), BF16), pltpu.SemaphoreType.DMA((width // COLUMNS,))],
    )
    last = lax.ppermute(next_sum, "dp", swap(4))
    up_got = lax.ppermute(up_away, "fsdp", swap(2))
    up_mine, *up_sent = call(
        up_sum_kernel, (struct((half, features), F32),) + (struct((half, features), BF16),) * 3, up_keep, up_got,
        us=UP_US,
    )
    up_last = [lax.ppermute(sent, "dp", swap(4, k + 1)) for k, sent in enumerate(up_sent)]

    input_gradient, other_second = base(first_rows, got_second, relay_second, input_first)
    base_send, base_keep = call(share_kernel, (struct((rows, features), F32),) * 2, own_out, other_first, other_second, lora)
    base_got = lax.ppermute(base_send, "tp", swap(2))
    value_output = call(total_kernel, struct((rows, features), BF16), base_keep, base_got)
    up_share = call(total_kernel, struct((half, features), F32), up_mine, *up_last, after=(base_send,))
    down_share = call(total_kernel, struct((half, width), F32), mine_sum, last, us=LAST_US)
    shares = [share.reshape(jobs, rank // 2, share.shape[1]) for share in (down_share, up_share)]
    return value_output, input_gradient, *shares


def dispatch_rows(
    tokens,
    output_gradient,
    frozen_value_weight,
    adapter_down_weight,
    adapter_up_weight,
    deal,
    row_local_job,
):
    row_count = tokens.shape[0]
    width_half = tokens.shape[1]
    jobs_owned_here = adapter_down_weight.shape[0]
    rank_extent = adapter_down_weight.shape[1]
    partial_value_rows = adapter_up_weight.shape[2]
    partner_count = lax.axis_size("dp")
    job_slot_count = 5 * row_count // (4 * partner_count)
    slot_total = partner_count * job_slot_count
    tp_index = lax.axis_index("tp")
    grad_part = lax.dynamic_slice_in_dim(
        output_gradient, tp_index * partial_value_rows, partial_value_rows, 1
    )
    contract_last = (((1,), (1,)), ((), ()))
    full_weight = lax.all_gather(frozen_value_weight, "fsdp", axis=1, tiled=True)
    frozen_output = jnp.dot(tokens, full_weight, preferred_element_type=jnp.float32)
    frozen_gradient = lax.dot_general(
        output_gradient, full_weight, contract_last, preferred_element_type=jnp.float32
    )
    value_share = lax.psum_scatter(frozen_output, "tp", scatter_dimension=1, tiled=True)
    row_dest = deal[:, 0]
    dest_onehot = (row_dest[:, None] == jnp.arange(partner_count, dtype=jnp.int32)[None, :]).astype(
        jnp.int32
    )
    earlier = jnp.cumsum(dest_onehot, axis=0) - dest_onehot
    slot_rank = jnp.sum(earlier * dest_onehot, axis=1)
    row_slot = row_dest * job_slot_count + slot_rank
    row_ids = jnp.arange(row_count, dtype=jnp.int32)
    slot_full = jnp.zeros((slot_total,), jnp.int32).at[row_slot].set(1)
    source_row = jnp.zeros((slot_total,), jnp.int32).at[row_slot].set(row_ids)
    is_full = slot_full > 0
    send_tokens = jnp.where(is_full[:, None], tokens[source_row], jnp.zeros((), jnp.bfloat16))
    send_grads = jnp.where(is_full[:, None], grad_part[source_row], jnp.zeros((), jnp.bfloat16))
    send_jobs = jnp.where(is_full, row_local_job[source_row], -1)
    got_tokens, got_grads, got_jobs = (
        lax.all_to_all(
            send_tokens.reshape(partner_count, job_slot_count, width_half),
            "dp",
            split_axis=0,
            concat_axis=0,
            tiled=True,
        ),
        lax.all_to_all(
            send_grads.reshape(partner_count, job_slot_count, partial_value_rows),
            "dp",
            split_axis=0,
            concat_axis=0,
            tiled=True,
        ),
        lax.all_to_all(
            send_jobs.reshape(partner_count, job_slot_count),
            "dp",
            split_axis=0,
            concat_axis=0,
            tiled=True,
        ),
    )
    got_tokens = got_tokens.reshape(slot_total, width_half)
    got_grads = got_grads.reshape(slot_total, partial_value_rows)
    got_jobs = got_jobs.reshape(slot_total)
    job_pick = got_jobs[:, None] == jnp.arange(jobs_owned_here, dtype=jnp.int32)[None, :]
    flat_down_weight = adapter_down_weight.reshape(jobs_owned_here * rank_extent, width_half)
    flat_up_weight = adapter_up_weight.reshape(jobs_owned_here * rank_extent, partial_value_rows)
    every_down = lax.dot_general(
        got_tokens, flat_down_weight, contract_last, preferred_element_type=jnp.float32
    )
    every_up = lax.dot_general(
        got_grads, flat_up_weight, contract_last, preferred_element_type=jnp.float32
    )
    pick_mask = job_pick.astype(jnp.float32)[:, :, None]
    low_partial = jnp.sum(
        every_down.reshape(slot_total, jobs_owned_here, rank_extent) * pick_mask, axis=1
    )
    grad_partial = jnp.sum(
        every_up.reshape(slot_total, jobs_owned_here, rank_extent) * pick_mask, axis=1
    )
    low_rank, grad_rank = lax.psum((low_partial, grad_partial), "tp")
    pick_narrow = job_pick.astype(jnp.bfloat16)[:, :, None]
    wide_rank_rows = (pick_narrow * low_rank.astype(jnp.bfloat16)[:, None, :]).reshape(
        slot_total, jobs_owned_here * rank_extent
    )
    wide_gradient = (pick_narrow * grad_rank.astype(jnp.bfloat16)[:, None, :]).reshape(
        slot_total, jobs_owned_here * rank_extent
    )
    adapter_output = (
        ADAPTER_SCALE * jnp.dot(wide_rank_rows, flat_up_weight, preferred_element_type=jnp.float32)
    ).astype(jnp.bfloat16)
    adapter_gradient = (
        ADAPTER_SCALE * jnp.dot(wide_gradient, flat_down_weight, preferred_element_type=jnp.float32)
    ).astype(jnp.bfloat16)
    contract_first = (((0,), (0,)), ((), ()))
    down_product = ADAPTER_SCALE * lax.dot_general(
        wide_gradient, got_tokens, contract_first, preferred_element_type=jnp.float32
    )
    up_product = ADAPTER_SCALE * lax.dot_general(
        wide_rank_rows, got_grads, contract_first, preferred_element_type=jnp.float32
    )
    down_share, up_share = (
        lax.psum_scatter(
            down_product.reshape(jobs_owned_here, rank_extent, width_half),
            "fsdp",
            scatter_dimension=1,
            tiled=True,
        ),
        lax.psum_scatter(
            up_product.reshape(jobs_owned_here, rank_extent, partial_value_rows),
            "fsdp",
            scatter_dimension=1,
            tiled=True,
        ),
    )
    back_out, back_grad = (
        lax.all_to_all(
            adapter_output.reshape(partner_count, job_slot_count, partial_value_rows),
            "dp",
            split_axis=0,
            concat_axis=0,
            tiled=True,
        ),
        lax.all_to_all(
            adapter_gradient.reshape(partner_count, job_slot_count, width_half),
            "dp",
            split_axis=0,
            concat_axis=0,
            tiled=True,
        ),
    )
    row_out = back_out.reshape(slot_total, partial_value_rows)[row_slot]
    row_grad = back_grad.reshape(slot_total, width_half)[row_slot]
    value_output = (value_share + row_out.astype(jnp.float32)).astype(jnp.bfloat16)
    input_gradient = (frozen_gradient + row_grad.astype(jnp.float32)).astype(jnp.bfloat16)
    return (value_output, input_gradient, down_share, up_share)


def solution(mesh):
    small = dict(mesh.shape) == {"rep": 2, "dp": 4, "fsdp": 2, "tp": 2}
    local = gather_adapters if small else dispatch_rows
    in_specs = (
        P(("rep", "dp", "fsdp"), "tp"),
        P(("rep", "dp", "fsdp"), None),
        P("tp", "fsdp"),
        P(("rep", "dp"), None, "tp"),
        P(("rep", "dp"), None, "tp"),
        P(("rep", "dp", "fsdp"), None),
        P(("rep", "dp", "fsdp")),
    )
    out_specs = (
        P(("rep", "dp", "fsdp"), "tp"),
        P(("rep", "dp", "fsdp"), "tp"),
        P(("rep", "dp"), "fsdp", "tp"),
        P(("rep", "dp"), "fsdp", "tp"),
    )
    return jax.shard_map(local, mesh=mesh, in_specs=in_specs, out_specs=out_specs, check_vma=False)
```

```python
import functools

import jax
import jax.numpy as jnp
from jax import lax
from jax.experimental import pallas as pl
from jax.experimental.pallas import tpu as pltpu
from jax.sharding import PartitionSpec as P

ADAPTER_SCALE = 2.0

BF16 = jnp.bfloat16
F32 = jnp.float32
PLAIN = (((1,), (0,)), ((), ()))
CONTRACT_LAST = (((1,), (1,)), ((), ()))
VMEM_BYTES = 10 * 1024 * 1024
COLUMNS = 1024
OWN_PARTS = 4
PART_US = 3.6
SEND_US = 6
FAR_US = 6
SUM_US = 6
NEAR_US = 6
UP_US = 4
LAST_US = 15
FIRST_SHARE = 4
WHOLE = pl.BlockSpec(memory_space=pltpu.VMEM)
ANY = pl.BlockSpec(memory_space=pl.ANY)
HBM = pl.BlockSpec(memory_space=pltpu.HBM)


def swap(extent, flip=1):
    return [(i, i ^ flip) for i in range(extent)]


def dot(left, right, dims=PLAIN):
    return lax.dot_general(left, right, dims, preferred_element_type=F32)


def struct(shape, dtype):
    return jax.ShapeDtypeStruct(shape, dtype)


def holders():
    here = lax.axis_index("dp")
    return here, here ^ 1, jnp.where(here < 2, 2, 1), jnp.where(here < 2, 3, 0)


def job_mask(span, rank, job_row):
    return lax.broadcasted_iota(jnp.int32, (span, job_row.shape[1]), 0) // rank == job_row


def prepare_kernel(gradient, deal, job, up, down, *refs):
    features = up.shape[1]
    start = pl.multiple_of(lax.axis_index("tp") * features, features)
    sources = gradient.at[:, pl.ds(start, features)], deal, job, up
    copies = [pltpu.make_async_copy(source, out, refs[4].at[k]) for k, (source, out) in enumerate(zip(sources, refs))]
    for copy in copies:
        copy.start()
    for copy in copies:
        copy.wait()


def grad_partial_kernel(rank, near, far, gradient, deal, job, out):
    here = lax.axis_index("dp")
    span = out.shape[0]
    part = gradient[...]
    owner = deal[...]
    total = jnp.zeros(out.shape, F32)
    for k in range(4):
        block = (near, far)[k // 2][k % 2 * span : (k % 2 + 1) * span]
        total += jnp.where(owner == (here ^ k), dot(block, part, CONTRACT_LAST), 0.0)
    out[...] = jnp.where(job_mask(span, rank, job[...]), total, 0.0)


def each_column(ref):
    def run(body):
        def step(i, carry):
            body(pl.ds(pl.multiple_of(i * COLUMNS, COLUMNS), COLUMNS))
            return carry

        lax.fori_loop(0, ref.shape[1] // COLUMNS, step, 0)

    return run


def half_rows(narrow, rank, which):
    half = rank // 2
    pick = [narrow[j * half : (j + 1) * half] for j in range(narrow.shape[0] // half)]
    low, high = jnp.concatenate(pick[0::2]), jnp.concatenate(pick[1::2])
    return jnp.where(which == 0, low, high)


def wide_rows(narrow, owner, names):
    return jnp.concatenate([jnp.where(owner == name, narrow, 0.0) for name in names]).astype(BF16)


def grad_send_kernel(rank, first, second, deal, tokens, rank_out, far_out, near_out):
    total = first[...] + second[...]
    rank_out[...] = total.astype(BF16)
    total = total.astype(BF16).astype(F32)
    sent = ADAPTER_SCALE * half_rows(total, rank, 1 - lax.axis_index("fsdp"))
    mine, beside, middle, end = holders()
    wide = wide_rows(sent, deal[...], (end, middle, beside, mine))
    split = far_out.shape[0]

    @each_column(tokens)
    def _(at):
        made = dot(wide, tokens[:, at])
        far_out[:, at] = made[:split].astype(BF16)
        near_out[:, at] = made[split:].astype(BF16)


def kept_rows(rank, grad_rank):
    return ADAPTER_SCALE * half_rows(grad_rank[...].astype(F32), rank, lax.axis_index("fsdp"))


def in_middle():
    here = lax.axis_index("dp")
    return (here == 1) | (here == 2)


def far_kernel(rank, got, grad_rank, deal, tokens, down_cross, out, swap_out):
    _, _, middle, end = holders()
    wide = wide_rows(kept_rows(rank, grad_rank), deal[...], (end, middle))

    @each_column(tokens)
    def _(at):
        made = (dot(wide, tokens[:, at]) + got[:, at].astype(F32)).astype(BF16)
        out[:, at] = made
        swap_out[:, at] = jnp.where(in_middle(), down_cross[:, at], made)


def near_kept_kernel(rank, grad_rank, deal, tokens, out):
    mine, beside, _, _ = holders()
    wide = wide_rows(kept_rows(rank, grad_rank), deal[...], (beside, mine))

    @each_column(tokens)
    def _(at):
        out[:, at] = dot(wide, tokens[:, at])


def near_kernel(kept, got, cross, next_out, mine_out):
    split = next_out.shape[0]

    @each_column(kept)
    def _(at):
        made = kept[:, at] + got[:, at].astype(F32) + cross[:, at].astype(F32)
        next_out[:, at] = made[:split].astype(BF16)
        mine_out[:, at] = made[split:]


def low_kernel(rank, names, blocks, *refs):
    tokens, deal, job = refs[:3]
    out = refs[-1]
    owner = deal[...]
    name = holders()
    started = len(refs) - 4 > sum(blocks)
    out[...] = jnp.zeros(out.shape, F32)

    @each_column(tokens)
    def _(at):
        left = list(refs[3:-1])
        total = out[...]
        for k, count in zip(names, blocks):
            block = left.pop(0)[:, at]
            if count == 2:
                block = jnp.where(in_middle(), block, left.pop(0)[:, at])
            total += jnp.where(owner == name[k], dot(block, tokens[:, at], CONTRACT_LAST), 0.0)
        out[...] = total

    out[...] = jnp.where(job_mask(out.shape[0], rank, job[...]), out[...], 0.0)
    if started:
        out[...] += refs[-2][...]


def up_kernel(rank, low, low_got, gradient, deal, near, far, keep_out, away_out, lora_out):
    here = lax.axis_index("dp")
    span = low.shape[0]
    half = span // 2
    narrow = (low[...] + low_got[...]).astype(BF16).astype(F32)
    owner = deal[...]
    part = gradient[...]
    wide = jnp.concatenate([jnp.where(owner == (here ^ k), narrow, 0.0) for k in range(4)])
    made = ADAPTER_SCALE * dot(wide.astype(BF16), part)
    side = lax.axis_index("fsdp")
    for k in range(4):
        block = made[k * span : (k + 1) * span]
        keep_out[k * half : (k + 1) * half] = half_rows(block, rank, side)
        away_out[k * half : (k + 1) * half] = half_rows(block, rank, 1 - side).astype(BF16)
    ups = jnp.concatenate([near[...], far[...]])
    lora_out[...] = ADAPTER_SCALE * dot(wide.T.astype(BF16), ups)


def up_sum_kernel(keep, got, mine, *sent):
    total = keep[...] + got[...].astype(F32)
    half = mine.shape[0]
    mine[...] = total[:half]
    for k, out in enumerate(sent):
        out[...] = total[(k + 1) * half : (k + 2) * half].astype(BF16)


def own_kernel(tokens, own, out, buffer, sems):
    count = own.shape[0] // OWN_PARTS
    copies = []
    for k in range(OWN_PARTS):
        at = pl.ds(k * count, count)
        copies.append(pltpu.make_async_copy(own.at[at], buffer.at[at], sems.at[k]))
        copies[-1].start()
    for k, copy in enumerate(copies):
        at = pl.ds(k * count, count)
        copy.wait()
        part = dot(tokens[:, at], buffer[at])
        out[...] = part if k == 0 else out[...] + part


def base_kernel(offset, gradient, grad_rank, deal, direct, relayed, *refs):
    downs, (tokens, own) = refs[:6], refs[6:8]
    grad_out, other_out, wide, buffer, own_in, token_in, sems, out_sems = refs[-8:]
    features = own.shape[1]
    count = direct.shape[0]
    mine = pl.multiple_of(lax.axis_index("fsdp") * features, features)
    other = pl.multiple_of((1 - lax.axis_index("fsdp")) * features, features)
    rep = lax.axis_index("rep")
    spots, copies, stores = [], [], []
    for side in range(2):
        start = (rep ^ side) * (own.shape[0] // 2) + offset
        spots.append(pl.ds(pl.multiple_of(start, 256), count))
        copies.append(
            [
                pltpu.make_async_copy(own.at[spots[side], :], own_in.at[side], sems.at[side, 0]),
                pltpu.make_async_copy(tokens.at[:, spots[side]], token_in.at[side], sems.at[side, 1]),
            ]
        )
        for copy in copies[side]:
            copy.start()
    narrow = ADAPTER_SCALE * grad_rank[...].astype(F32)
    wide[...] = jnp.concatenate([jnp.where(deal[...] == name, narrow, 0.0) for name in holders()]).T.astype(BF16)
    for side, (at, weight) in enumerate(zip(spots, (direct, relayed))):
        parts = [down[:, at] for down in downs]
        parts[2:] = [jnp.where(in_middle(), parts[k], parts[k + 1]) for k in (2, 4)]
        total = dot(wide[...], jnp.concatenate(parts))
        total += dot(gradient[:, pl.ds(other, features)], weight[...], CONTRACT_LAST)
        copies[side][0].wait()
        total += dot(gradient[:, pl.ds(mine, features)], own_in[side], CONTRACT_LAST)
        buffer[side] = total.astype(BF16)
        stores.append(pltpu.make_async_copy(buffer.at[side], grad_out.at[:, at], out_sems.at[side]))
        stores[side].start()
        copies[side][1].wait()
        other_part = dot(token_in[side], weight[...])
        other_out[...] = other_part if side == 0 else other_out[...] + other_part
    for store in stores:
        store.wait()


def call(kernel, out_shape, *args, after=(), in_specs=None, out_specs=None, us=0, **more):
    count = len(args)
    if out_specs is None:
        out_specs = (WHOLE,) * len(out_shape) if isinstance(out_shape, tuple) else WHOLE
    if after:
        inner = kernel
        kernel = lambda *refs: inner(*refs[:count], *refs[count + len(after) :])
    return pl.pallas_call(
        kernel,
        out_shape=out_shape,
        in_specs=(in_specs or [WHOLE] * count) + [ANY] * len(after),
        out_specs=out_specs,
        compiler_params=pltpu.CompilerParams(vmem_limit_bytes=VMEM_BYTES),
        cost_estimate=pl.CostEstimate(flops=int(us * 1.15e9), bytes_accessed=0, transcendentals=0) if us else None,
        **more,
    )(*args, *after)


def cut_kernel(weight, first, second, sems):
    half = weight.shape[0] // 2
    start = pl.multiple_of(lax.axis_index("rep") * half, half)
    count = first.shape[0]
    copies = [
        pltpu.make_async_copy(weight.at[pl.ds(start, count)], first, sems.at[0]),
        pltpu.make_async_copy(weight.at[pl.ds(start + count, half - count)], second, sems.at[1]),
    ]
    for copy in copies:
        copy.start()
    for copy in copies:
        copy.wait()


def join_kernel(one, two, out):
    half = one.shape[0]
    out[:half] = one[...]
    out[half:] = two[...]


def share_kernel(own, first, second, lora, send_out, keep_out):
    other = first[...] + second[...]
    same = lax.axis_index("fsdp") == lax.axis_index("tp")
    send_out[...] = jnp.where(same, other, own[...])
    keep_out[...] = jnp.where(same, own[...], other) + lora[...]


def total_kernel(*refs):
    total = refs[0][...]
    for ref in refs[1:-1]:
        total += ref[...].astype(F32)
    refs[-1][...] = total.astype(refs[-1].dtype)


def finish_kernel(base_keep, base_got, mine, last, up_mine, one, two, three, value_out, down_out, up_out):
    total_kernel(base_keep, base_got, value_out)
    total_kernel(up_mine, one, two, three, up_out)
    down_out[...] = mine[...] + last[...].astype(F32)


def add_kernel(one, two, out):
    out[...] = (one[...].astype(F32) + two[...].astype(F32)).astype(BF16)


def ordered(value, before):
    return lax.optimization_barrier((value, before))[0]


def gather_adapters(
    tokens,
    output_gradient,
    frozen_value_weight,
    adapter_down_weight,
    adapter_up_weight,
    deal,
    row_local_job,
):
    rows, width = tokens.shape
    jobs, rank, features = adapter_up_weight.shape
    span = jobs * rank
    half = span // 2
    down = adapter_down_weight.reshape(span, width)
    up = adapter_up_weight.reshape(span, features)
    deal = deal.reshape(1, rows)
    job = row_local_job.reshape(1, rows)
    first_rows = width * FIRST_SHARE // 16
    outward, middle = [(1, 0), (2, 3)], [(1, 2), (2, 1)]

    up_got_first = lax.ppermute(up, "dp", swap(4))
    row = struct((1, rows), jnp.int32)
    grad_mine, deal, job, up = call(
        prepare_kernel, (struct((rows, features), BF16), row, row, struct((span, features), BF16)),
        output_gradient, deal, job, up, down,
        in_specs=[ANY] * 4 + [WHOLE], scratch_shapes=[pltpu.SemaphoreType.DMA((4,))],
    )
    up_pair = call(join_kernel, struct((2 * span, features), BF16), up, up_got_first, after=(grad_mine,))
    ups = up_pair, lax.ppermute(up_pair, "dp", swap(4, 2))
    weight_first, weight_second = call(
        cut_kernel,
        (struct((first_rows, features), BF16), struct((width // 2 - first_rows, features), BF16)),
        frozen_value_weight,
        in_specs=[HBM],
        out_specs=(ANY, ANY),
        scratch_shapes=[pltpu.SemaphoreType.DMA((2,))],
    )
    got_first = lax.ppermute(weight_first, "fsdp", swap(2))

    narrow = struct((span, rows), F32)
    half_wide = struct((half, width), BF16)
    span_wide = struct((span, width), BF16)
    grad_part = call(functools.partial(grad_partial_kernel, rank), narrow, *ups, grad_mine, deal, job, us=PART_US)
    grad_got = lax.ppermute(grad_part, "tp", swap(2))
    grad_rank, send_far, send_near = call(
        functools.partial(grad_send_kernel, rank), (struct((span, rows), BF16), span_wide, span_wide),
        grad_part, grad_got, deal, tokens, after=(got_first,), us=SEND_US,
    )
    down_sent = ordered(down, grad_part)
    down_next = lax.ppermute(down_sent, "dp", swap(4))
    down_cross = lax.ppermute(ordered(down, grad_part), "dp", middle)
    got_far = lax.ppermute(send_far, "fsdp", swap(2))
    own_out = call(
        own_kernel,
        struct((rows, features), F32),
        tokens,
        frozen_value_weight,
        after=(send_far,),
        in_specs=[WHOLE, HBM],
        scratch_shapes=[pltpu.VMEM((width, features), BF16), pltpu.SemaphoreType.DMA((OWN_PARTS,))],
    )
    relay_first = lax.ppermute(ordered(got_first, own_out), "rep", swap(2))
    near_kept = call(
        functools.partial(near_kept_kernel, rank), struct((span, width), F32), grad_rank, deal, tokens
    )
    far, far_swap = call(
        functools.partial(far_kernel, rank), (span_wide, span_wide),
        got_far, grad_rank, deal, tokens, down_cross, after=(own_out, down_next, near_kept), us=FAR_US,
    )
    got_second = lax.ppermute(ordered(weight_second, got_far), "fsdp", swap(2))
    swapped = lax.ppermute(far_swap, "dp", swap(4))
    down_cross2 = lax.ppermute(ordered(down_next, down_cross), "dp", middle)
    low_near = call(
        functools.partial(low_kernel, rank, (0, 1), (1, 1)),
        narrow, tokens, deal, job, down, down_next, after=(far,),
    )
    low_first = call(
        functools.partial(low_kernel, rank, (2,), (2,)),
        narrow, tokens, deal, job, down_cross, swapped, low_near,
    )
    far_sum = call(add_kernel, span_wide, far, swapped, after=(down_cross2, low_near,), us=SUM_US)
    got_near = lax.ppermute(ordered(send_near, far), "fsdp", swap(2))
    cross = lax.ppermute(far_sum, "dp", middle)
    down_out2 = lax.ppermute(ordered(down_cross2, far), "dp", outward)
    relay_second = lax.ppermute(ordered(got_second, far_sum), "rep", swap(2))
    low_part = call(
        functools.partial(low_kernel, rank, (3,), (2,)), narrow, tokens, deal, job, down_cross2, down_out2, low_first, after=()
    )
    low_got = lax.ppermute(low_part, "tp", swap(2))
    up_half = struct((4 * half, features), F32), struct((4 * half, features), BF16)
    up_keep, up_away, lora = call(
        functools.partial(up_kernel, rank), (*up_half, struct((rows, features), F32)),
        low_part, low_got, grad_mine, deal, *ups,
    )
    def base(offset, direct, relayed, *into):
        count = direct.shape[0]
        return call(
            functools.partial(base_kernel, offset),
            (struct((rows, width), BF16), struct((rows, features), F32)),
            output_gradient, grad_rank, deal, direct, relayed,
            down, down_next, down_cross, swapped, down_cross2, down_out2, tokens, frozen_value_weight,
            after=into,
            in_specs=[WHOLE] * 11 + [HBM] * 2,
            out_specs=(HBM, WHOLE),
            scratch_shapes=[
                pltpu.VMEM((rows, 4 * span), BF16),
                pltpu.VMEM((2, rows, count), BF16),
                pltpu.VMEM((2, count, features), BF16),
                pltpu.VMEM((2, rows, count), BF16),
                pltpu.SemaphoreType.DMA((2, 2)),
                pltpu.SemaphoreType.DMA((2,)),
            ],
            input_output_aliases={13: 0} if into else {},
        )

    input_first, other_first = base(0, got_first, relay_first)
    input_gradient, other_second = base(first_rows, got_second, relay_second, input_first)
    next_sum, mine_sum = call(
        near_kernel, (half_wide, struct((half, width), F32)),
        near_kept, got_near, cross, after=(up_away, other_first, relay_second), us=NEAR_US,
    )
    last = lax.ppermute(next_sum, "dp", swap(4))
    up_got = lax.ppermute(up_away, "fsdp", swap(2))
    up_mine, *up_sent = call(
        up_sum_kernel, (struct((half, features), F32),) + (struct((half, features), BF16),) * 3, up_keep, up_got,
        us=UP_US,
    )
    up_last = [lax.ppermute(sent, "dp", swap(4, k + 1)) for k, sent in enumerate(up_sent)]

    base_send, base_keep = call(share_kernel, (struct((rows, features), F32),) * 2, own_out, other_first, other_second, lora)
    base_got = lax.ppermute(base_send, "tp", swap(2))
    value_output, down_share, up_share = call(
        finish_kernel,
        (struct((rows, features), BF16), struct((half, width), F32), struct((half, features), F32)),
        base_keep, base_got, mine_sum, last, up_mine, *up_last, us=LAST_US,
    )
    shares = [share.reshape(jobs, rank // 2, share.shape[1]) for share in (down_share, up_share)]
    return value_output, input_gradient, *shares


def dispatch_rows(
    tokens,
    output_gradient,
    frozen_value_weight,
    adapter_down_weight,
    adapter_up_weight,
    deal,
    row_local_job,
):
    row_count = tokens.shape[0]
    width_half = tokens.shape[1]
    jobs_owned_here = adapter_down_weight.shape[0]
    rank_extent = adapter_down_weight.shape[1]
    partial_value_rows = adapter_up_weight.shape[2]
    partner_count = lax.axis_size("dp")
    job_slot_count = 5 * row_count // (4 * partner_count)
    slot_total = partner_count * job_slot_count
    tp_index = lax.axis_index("tp")
    grad_part = lax.dynamic_slice_in_dim(
        output_gradient, tp_index * partial_value_rows, partial_value_rows, 1
    )
    contract_last = (((1,), (1,)), ((), ()))
    full_weight = lax.all_gather(frozen_value_weight, "fsdp", axis=1, tiled=True)
    frozen_output = jnp.dot(tokens, full_weight, preferred_element_type=jnp.float32)
    frozen_gradient = lax.dot_general(
        output_gradient, full_weight, contract_last, preferred_element_type=jnp.float32
    )
    value_share = lax.psum_scatter(frozen_output, "tp", scatter_dimension=1, tiled=True)
    row_dest = deal[:, 0]
    dest_onehot = (row_dest[:, None] == jnp.arange(partner_count, dtype=jnp.int32)[None, :]).astype(
        jnp.int32
    )
    earlier = jnp.cumsum(dest_onehot, axis=0) - dest_onehot
    slot_rank = jnp.sum(earlier * dest_onehot, axis=1)
    row_slot = row_dest * job_slot_count + slot_rank
    row_ids = jnp.arange(row_count, dtype=jnp.int32)
    slot_full = jnp.zeros((slot_total,), jnp.int32).at[row_slot].set(1)
    source_row = jnp.zeros((slot_total,), jnp.int32).at[row_slot].set(row_ids)
    is_full = slot_full > 0
    send_tokens = jnp.where(is_full[:, None], tokens[source_row], jnp.zeros((), jnp.bfloat16))
    send_grads = jnp.where(is_full[:, None], grad_part[source_row], jnp.zeros((), jnp.bfloat16))
    send_jobs = jnp.where(is_full, row_local_job[source_row], -1)
    got_tokens, got_grads, got_jobs = (
        lax.all_to_all(
            send_tokens.reshape(partner_count, job_slot_count, width_half),
            "dp",
            split_axis=0,
            concat_axis=0,
            tiled=True,
        ),
        lax.all_to_all(
            send_grads.reshape(partner_count, job_slot_count, partial_value_rows),
            "dp",
            split_axis=0,
            concat_axis=0,
            tiled=True,
        ),
        lax.all_to_all(
            send_jobs.reshape(partner_count, job_slot_count),
            "dp",
            split_axis=0,
            concat_axis=0,
            tiled=True,
        ),
    )
    got_tokens = got_tokens.reshape(slot_total, width_half)
    got_grads = got_grads.reshape(slot_total, partial_value_rows)
    got_jobs = got_jobs.reshape(slot_total)
    job_pick = got_jobs[:, None] == jnp.arange(jobs_owned_here, dtype=jnp.int32)[None, :]
    flat_down_weight = adapter_down_weight.reshape(jobs_owned_here * rank_extent, width_half)
    flat_up_weight = adapter_up_weight.reshape(jobs_owned_here * rank_extent, partial_value_rows)
    every_down = lax.dot_general(
        got_tokens, flat_down_weight, contract_last, preferred_element_type=jnp.float32
    )
    every_up = lax.dot_general(
        got_grads, flat_up_weight, contract_last, preferred_element_type=jnp.float32
    )
    pick_mask = job_pick.astype(jnp.float32)[:, :, None]
    low_partial = jnp.sum(
        every_down.reshape(slot_total, jobs_owned_here, rank_extent) * pick_mask, axis=1
    )
    grad_partial = jnp.sum(
        every_up.reshape(slot_total, jobs_owned_here, rank_extent) * pick_mask, axis=1
    )
    low_rank, grad_rank = lax.psum((low_partial, grad_partial), "tp")
    pick_narrow = job_pick.astype(jnp.bfloat16)[:, :, None]
    wide_rank_rows = (pick_narrow * low_rank.astype(jnp.bfloat16)[:, None, :]).reshape(
        slot_total, jobs_owned_here * rank_extent
    )
    wide_gradient = (pick_narrow * grad_rank.astype(jnp.bfloat16)[:, None, :]).reshape(
        slot_total, jobs_owned_here * rank_extent
    )
    adapter_output = (
        ADAPTER_SCALE * jnp.dot(wide_rank_rows, flat_up_weight, preferred_element_type=jnp.float32)
    ).astype(jnp.bfloat16)
    adapter_gradient = (
        ADAPTER_SCALE * jnp.dot(wide_gradient, flat_down_weight, preferred_element_type=jnp.float32)
    ).astype(jnp.bfloat16)
    contract_first = (((0,), (0,)), ((), ()))
    down_product = ADAPTER_SCALE * lax.dot_general(
        wide_gradient, got_tokens, contract_first, preferred_element_type=jnp.float32
    )
    up_product = ADAPTER_SCALE * lax.dot_general(
        wide_rank_rows, got_grads, contract_first, preferred_element_type=jnp.float32
    )
    down_share, up_share = (
        lax.psum_scatter(
            down_product.reshape(jobs_owned_here, rank_extent, width_half),
            "fsdp",
            scatter_dimension=1,
            tiled=True,
        ),
        lax.psum_scatter(
            up_product.reshape(jobs_owned_here, rank_extent, partial_value_rows),
            "fsdp",
            scatter_dimension=1,
            tiled=True,
        ),
    )
    back_out, back_grad = (
        lax.all_to_all(
            adapter_output.reshape(partner_count, job_slot_count, partial_value_rows),
            "dp",
            split_axis=0,
            concat_axis=0,
            tiled=True,
        ),
        lax.all_to_all(
            adapter_gradient.reshape(partner_count, job_slot_count, width_half),
            "dp",
            split_axis=0,
            concat_axis=0,
            tiled=True,
        ),
    )
    row_out = back_out.reshape(slot_total, partial_value_rows)[row_slot]
    row_grad = back_grad.reshape(slot_total, width_half)[row_slot]
    value_output = (value_share + row_out.astype(jnp.float32)).astype(jnp.bfloat16)
    input_gradient = (frozen_gradient + row_grad.astype(jnp.float32)).astype(jnp.bfloat16)
    return (value_output, input_gradient, down_share, up_share)


def solution(mesh):
    small = dict(mesh.shape) == {"rep": 2, "dp": 4, "fsdp": 2, "tp": 2}
    local = gather_adapters if small else dispatch_rows
    in_specs = (
        P(("rep", "dp", "fsdp"), "tp"),
        P(("rep", "dp", "fsdp"), None),
        P("tp", "fsdp"),
        P(("rep", "dp"), None, "tp"),
        P(("rep", "dp"), None, "tp"),
        P(("rep", "dp", "fsdp"), None),
        P(("rep", "dp", "fsdp")),
    )
    out_specs = (
        P(("rep", "dp", "fsdp"), "tp"),
        P(("rep", "dp", "fsdp"), "tp"),
        P(("rep", "dp"), "fsdp", "tp"),
        P(("rep", "dp"), "fsdp", "tp"),
    )
    return jax.shard_map(local, mesh=mesh, in_specs=in_specs, out_specs=out_specs, check_vma=False)
```

```python
import functools

import jax
import jax.numpy as jnp
from jax import lax
from jax.experimental import pallas as pl
from jax.experimental.pallas import tpu as pltpu
from jax.sharding import PartitionSpec as P

ADAPTER_SCALE = 2.0

BF16 = jnp.bfloat16
F32 = jnp.float32
PLAIN = (((1,), (0,)), ((), ()))
CONTRACT_LAST = (((1,), (1,)), ((), ()))
VMEM_BYTES = 10 * 1024 * 1024
COLUMNS = 1024
OWN_PARTS = 4
PART_US = 3.6
SEND_US = 6
FAR_US = 6
SUM_US = 6
NEAR_US = 6
UP_US = 4
LAST_US = 15
MARK_US = 3
FIRST_SHARE = 4
WHOLE = pl.BlockSpec(memory_space=pltpu.VMEM)
ANY = pl.BlockSpec(memory_space=pl.ANY)
HBM = pl.BlockSpec(memory_space=pltpu.HBM)


def swap(extent, flip=1):
    return [(i, i ^ flip) for i in range(extent)]


def dot(left, right, dims=PLAIN):
    return lax.dot_general(left, right, dims, preferred_element_type=F32)


def struct(shape, dtype):
    return jax.ShapeDtypeStruct(shape, dtype)


def holders():
    here = lax.axis_index("dp")
    return here, here ^ 1, jnp.where(here < 2, 2, 1), jnp.where(here < 2, 3, 0)


def job_mask(span, rank, job_row):
    return lax.broadcasted_iota(jnp.int32, (span, job_row.shape[1]), 0) // rank == job_row


def prepare_kernel(gradient, deal, job, up, down, *refs):
    features = up.shape[1]
    start = pl.multiple_of(lax.axis_index("tp") * features, features)
    sources = gradient.at[:, pl.ds(start, features)], deal, job, up
    copies = [pltpu.make_async_copy(source, out, refs[4].at[k]) for k, (source, out) in enumerate(zip(sources, refs))]
    for copy in copies:
        copy.start()
    for copy in copies:
        copy.wait()


def grad_partial_kernel(rank, near, far, gradient, deal, job, out):
    here = lax.axis_index("dp")
    span = out.shape[0]
    part = gradient[...]
    owner = deal[...]
    total = jnp.zeros(out.shape, F32)
    for k in range(4):
        block = (near, far)[k // 2][k % 2 * span : (k % 2 + 1) * span]
        total += jnp.where(owner == (here ^ k), dot(block, part, CONTRACT_LAST), 0.0)
    out[...] = jnp.where(job_mask(span, rank, job[...]), total, 0.0)


def each_column(ref):
    def run(body):
        def step(i, carry):
            body(pl.ds(pl.multiple_of(i * COLUMNS, COLUMNS), COLUMNS))
            return carry

        lax.fori_loop(0, ref.shape[1] // COLUMNS, step, 0)

    return run


def half_rows(narrow, rank, which):
    half = rank // 2
    pick = [narrow[j * half : (j + 1) * half] for j in range(narrow.shape[0] // half)]
    low, high = jnp.concatenate(pick[0::2]), jnp.concatenate(pick[1::2])
    return jnp.where(which == 0, low, high)


def wide_rows(narrow, owner, names):
    return jnp.concatenate([jnp.where(owner == name, narrow, 0.0) for name in names]).astype(BF16)


def grad_send_kernel(rank, first, second, deal, tokens, rank_out, far_out, near_out):
    total = first[...] + second[...]
    rank_out[...] = total.astype(BF16)
    total = total.astype(BF16).astype(F32)
    sent = ADAPTER_SCALE * half_rows(total, rank, 1 - lax.axis_index("fsdp"))
    mine, beside, middle, end = holders()
    wide = wide_rows(sent, deal[...], (end, middle, beside, mine))
    split = far_out.shape[0]

    @each_column(tokens)
    def _(at):
        made = dot(wide, tokens[:, at])
        far_out[:, at] = made[:split].astype(BF16)
        near_out[:, at] = made[split:].astype(BF16)


def kept_rows(rank, grad_rank):
    return ADAPTER_SCALE * half_rows(grad_rank[...].astype(F32), rank, lax.axis_index("fsdp"))


def in_middle():
    here = lax.axis_index("dp")
    return (here == 1) | (here == 2)


def far_kernel(rank, got, grad_rank, deal, tokens, down_cross, out, swap_out):
    _, _, middle, end = holders()
    wide = wide_rows(kept_rows(rank, grad_rank), deal[...], (end, middle))

    @each_column(tokens)
    def _(at):
        made = (dot(wide, tokens[:, at]) + got[:, at].astype(F32)).astype(BF16)
        out[:, at] = made
        swap_out[:, at] = jnp.where(in_middle(), down_cross[:, at], made)


def near_kept_kernel(rank, grad_rank, deal, tokens, out):
    mine, beside, _, _ = holders()
    wide = wide_rows(kept_rows(rank, grad_rank), deal[...], (beside, mine))

    @each_column(tokens)
    def _(at):
        out[:, at] = dot(wide, tokens[:, at])


def near_kernel(kept, got, cross, next_out, mine_out):
    split = next_out.shape[0]

    @each_column(kept)
    def _(at):
        made = kept[:, at] + got[:, at].astype(F32) + cross[:, at].astype(F32)
        next_out[:, at] = made[:split].astype(BF16)
        mine_out[:, at] = made[split:]


def low_kernel(rank, names, blocks, *refs):
    tokens, deal, job = refs[:3]
    out = refs[-1]
    owner = deal[...]
    name = holders()
    started = len(refs) - 4 > sum(blocks)
    out[...] = jnp.zeros(out.shape, F32)

    @each_column(tokens)
    def _(at):
        left = list(refs[3:-1])
        total = out[...]
        for k, count in zip(names, blocks):
            block = left.pop(0)[:, at]
            if count == 2:
                block = jnp.where(in_middle(), block, left.pop(0)[:, at])
            total += jnp.where(owner == name[k], dot(block, tokens[:, at], CONTRACT_LAST), 0.0)
        out[...] = total

    out[...] = jnp.where(job_mask(out.shape[0], rank, job[...]), out[...], 0.0)
    if started:
        out[...] += refs[-2][...]


def up_kernel(rank, low, low_got, gradient, deal, near, far, keep_out, away_out, lora_out):
    here = lax.axis_index("dp")
    span = low.shape[0]
    half = span // 2
    narrow = (low[...] + low_got[...]).astype(BF16).astype(F32)
    owner = deal[...]
    part = gradient[...]
    wide = jnp.concatenate([jnp.where(owner == (here ^ k), narrow, 0.0) for k in range(4)])
    made = ADAPTER_SCALE * dot(wide.astype(BF16), part)
    side = lax.axis_index("fsdp")
    for k in range(4):
        block = made[k * span : (k + 1) * span]
        keep_out[k * half : (k + 1) * half] = half_rows(block, rank, side)
        away_out[k * half : (k + 1) * half] = half_rows(block, rank, 1 - side).astype(BF16)
    ups = jnp.concatenate([near[...], far[...]])
    lora_out[...] = ADAPTER_SCALE * dot(wide.T.astype(BF16), ups)


def up_sum_kernel(keep, got, mine, *sent):
    total = keep[...] + got[...].astype(F32)
    half = mine.shape[0]
    mine[...] = total[:half]
    for k, out in enumerate(sent):
        out[...] = total[(k + 1) * half : (k + 2) * half].astype(BF16)


def own_kernel(tokens, own, out, buffer, sems):
    count = own.shape[0] // OWN_PARTS
    copies = []
    for k in range(OWN_PARTS):
        at = pl.ds(k * count, count)
        copies.append(pltpu.make_async_copy(own.at[at], buffer.at[at], sems.at[k]))
        copies[-1].start()
    for k, copy in enumerate(copies):
        at = pl.ds(k * count, count)
        copy.wait()
        part = dot(tokens[:, at], buffer[at])
        out[...] = part if k == 0 else out[...] + part


def base_kernel(offset, gradient, grad_rank, deal, direct, relayed, *refs):
    downs, (tokens, own) = refs[:6], refs[6:8]
    grad_out, other_out, wide, buffer, own_in, token_in, sems, out_sems = refs[-8:]
    features = own.shape[1]
    count = direct.shape[0]
    mine = pl.multiple_of(lax.axis_index("fsdp") * features, features)
    other = pl.multiple_of((1 - lax.axis_index("fsdp")) * features, features)
    rep = lax.axis_index("rep")
    spots, copies, stores = [], [], []
    for side in range(2):
        start = (rep ^ side) * (own.shape[0] // 2) + offset
        spots.append(pl.ds(pl.multiple_of(start, 256), count))
        copies.append(
            [
                pltpu.make_async_copy(own.at[spots[side], :], own_in.at[side], sems.at[side, 0]),
                pltpu.make_async_copy(tokens.at[:, spots[side]], token_in.at[side], sems.at[side, 1]),
            ]
        )
        for copy in copies[side]:
            copy.start()
    narrow = ADAPTER_SCALE * grad_rank[...].astype(F32)
    wide[...] = jnp.concatenate([jnp.where(deal[...] == name, narrow, 0.0) for name in holders()]).T.astype(BF16)
    for side, (at, weight) in enumerate(zip(spots, (direct, relayed))):
        parts = [down[:, at] for down in downs]
        parts[2:] = [jnp.where(in_middle(), parts[k], parts[k + 1]) for k in (2, 4)]
        total = dot(wide[...], jnp.concatenate(parts))
        total += dot(gradient[:, pl.ds(other, features)], weight[...], CONTRACT_LAST)
        copies[side][0].wait()
        total += dot(gradient[:, pl.ds(mine, features)], own_in[side], CONTRACT_LAST)
        buffer[side] = total.astype(BF16)
        stores.append(pltpu.make_async_copy(buffer.at[side], grad_out.at[:, at], out_sems.at[side]))
        stores[side].start()
        copies[side][1].wait()
        other_part = dot(token_in[side], weight[...])
        other_out[...] = other_part if side == 0 else other_out[...] + other_part
    for store in stores:
        store.wait()


def call(kernel, out_shape, *args, after=(), in_specs=None, out_specs=None, us=0, **more):
    count = len(args)
    if out_specs is None:
        out_specs = (WHOLE,) * len(out_shape) if isinstance(out_shape, tuple) else WHOLE
    if after:
        inner = kernel
        kernel = lambda *refs: inner(*refs[:count], *refs[count + len(after) :])
    return pl.pallas_call(
        kernel,
        out_shape=out_shape,
        in_specs=(in_specs or [WHOLE] * count) + [ANY] * len(after),
        out_specs=out_specs,
        compiler_params=pltpu.CompilerParams(vmem_limit_bytes=VMEM_BYTES),
        cost_estimate=pl.CostEstimate(flops=int(us * 1.15e9), bytes_accessed=0, transcendentals=0) if us else None,
        **more,
    )(*args, *after)


def cut_kernel(weight, first, second, sems):
    half = weight.shape[0] // 2
    start = pl.multiple_of(lax.axis_index("rep") * half, half)
    count = first.shape[0]
    copies = [
        pltpu.make_async_copy(weight.at[pl.ds(start, count)], first, sems.at[0]),
        pltpu.make_async_copy(weight.at[pl.ds(start + count, half - count)], second, sems.at[1]),
    ]
    for copy in copies:
        copy.start()
    for copy in copies:
        copy.wait()


def join_kernel(one, two, out):
    half = one.shape[0]
    out[:half] = one[...]
    out[half:] = two[...]


def share_kernel(own, first, second, lora, send_out, keep_out):
    other = first[...] + second[...]
    same = lax.axis_index("fsdp") == lax.axis_index("tp")
    send_out[...] = jnp.where(same, other, own[...])
    keep_out[...] = jnp.where(same, own[...], other) + lora[...]


def total_kernel(*refs):
    total = refs[0][...]
    for ref in refs[1:-1]:
        total += ref[...].astype(F32)
    refs[-1][...] = total.astype(refs[-1].dtype)


def finish_kernel(base_keep, base_got, mine, last, up_mine, one, two, three, value_out, down_out, up_out):
    total_kernel(base_keep, base_got, value_out)
    total_kernel(up_mine, one, two, three, up_out)
    down_out[...] = mine[...] + last[...].astype(F32)


def mark_kernel(out):
    out[...] = jnp.zeros(out.shape, out.dtype)


def add_kernel(one, two, out):
    out[...] = (one[...].astype(F32) + two[...].astype(F32)).astype(BF16)


def ordered(value, before):
    return lax.optimization_barrier((value, before))[0]


def gather_adapters(
    tokens,
    output_gradient,
    frozen_value_weight,
    adapter_down_weight,
    adapter_up_weight,
    deal,
    row_local_job,
):
    rows, width = tokens.shape
    jobs, rank, features = adapter_up_weight.shape
    span = jobs * rank
    half = span // 2
    down = adapter_down_weight.reshape(span, width)
    up = adapter_up_weight.reshape(span, features)
    deal = deal.reshape(1, rows)
    job = row_local_job.reshape(1, rows)
    first_rows = width * FIRST_SHARE // 16
    outward, middle = [(1, 0), (2, 3)], [(1, 2), (2, 1)]

    up_got_first = lax.ppermute(up, "dp", swap(4))
    row = struct((1, rows), jnp.int32)
    grad_mine, deal, job, up = call(
        prepare_kernel, (struct((rows, features), BF16), row, row, struct((span, features), BF16)),
        output_gradient, deal, job, up, down,
        in_specs=[ANY] * 4 + [WHOLE], scratch_shapes=[pltpu.SemaphoreType.DMA((4,))],
    )
    up_pair = call(join_kernel, struct((2 * span, features), BF16), up, up_got_first, after=(grad_mine,))
    ups = up_pair, lax.ppermute(up_pair, "dp", swap(4, 2))
    weight_first, weight_second = call(
        cut_kernel,
        (struct((first_rows, features), BF16), struct((width // 2 - first_rows, features), BF16)),
        frozen_value_weight,
        in_specs=[HBM],
        out_specs=(ANY, ANY),
        scratch_shapes=[pltpu.SemaphoreType.DMA((2,))],
    )
    got_first = lax.ppermute(weight_first, "fsdp", swap(2))

    narrow = struct((span, rows), F32)
    half_wide = struct((half, width), BF16)
    span_wide = struct((span, width), BF16)
    grad_part = call(functools.partial(grad_partial_kernel, rank), narrow, *ups, grad_mine, deal, job, us=PART_US)
    grad_got = lax.ppermute(grad_part, "tp", swap(2))
    grad_rank, send_far, send_near = call(
        functools.partial(grad_send_kernel, rank), (struct((span, rows), BF16), span_wide, span_wide),
        grad_part, grad_got, deal, tokens, after=(got_first,), us=SEND_US,
    )
    down_sent = ordered(down, grad_part)
    down_next = lax.ppermute(down_sent, "dp", swap(4))
    down_cross = lax.ppermute(ordered(down, grad_part), "dp", middle)
    got_far = lax.ppermute(send_far, "fsdp", swap(2))
    own_out = call(
        own_kernel,
        struct((rows, features), F32),
        tokens,
        frozen_value_weight,
        after=(send_far,),
        in_specs=[WHOLE, HBM],
        scratch_shapes=[pltpu.VMEM((width, features), BF16), pltpu.SemaphoreType.DMA((OWN_PARTS,))],
    )
    relay_first = lax.ppermute(ordered(got_first, own_out), "rep", swap(2))
    near_kept = call(
        functools.partial(near_kept_kernel, rank), struct((span, width), F32), grad_rank, deal, tokens
    )
    far, far_swap = call(
        functools.partial(far_kernel, rank), (span_wide, span_wide),
        got_far, grad_rank, deal, tokens, down_cross, after=(own_out, down_next, near_kept), us=FAR_US,
    )
    got_second = lax.ppermute(ordered(weight_second, got_far), "fsdp", swap(2))
    swapped = lax.ppermute(far_swap, "dp", swap(4))
    down_cross2 = lax.ppermute(ordered(down_next, down_cross), "dp", middle)
    low_near = call(
        functools.partial(low_kernel, rank, (0, 1), (1, 1)),
        narrow, tokens, deal, job, down, down_next, after=(far,),
    )
    low_first = call(
        functools.partial(low_kernel, rank, (2,), (2,)),
        narrow, tokens, deal, job, down_cross, swapped, low_near,
    )
    far_sum = call(add_kernel, span_wide, far, swapped, after=(down_cross2, low_near, relay_first), us=SUM_US)
    got_near = lax.ppermute(ordered(send_near, far), "fsdp", swap(2))
    cross = lax.ppermute(far_sum, "dp", middle)
    down_out2 = lax.ppermute(ordered(down_cross2, far), "dp", outward)
    relay_second = lax.ppermute(ordered(got_second, far_sum), "rep", swap(2))
    low_part = call(
        functools.partial(low_kernel, rank, (3,), (2,)), narrow, tokens, deal, job, down_cross2, down_out2, low_first, after=()
    )
    low_got = lax.ppermute(low_part, "tp", swap(2))
    up_half = struct((4 * half, features), F32), struct((4 * half, features), BF16)
    up_keep, up_away, lora = call(
        functools.partial(up_kernel, rank), (*up_half, struct((rows, features), F32)),
        low_part, low_got, grad_mine, deal, *ups,
    )
    def base(offset, direct, relayed, *into):
        count = direct.shape[0]
        return call(
            functools.partial(base_kernel, offset),
            (struct((rows, width), BF16), struct((rows, features), F32)),
            output_gradient, grad_rank, deal, direct, relayed,
            down, down_next, down_cross, swapped, down_cross2, down_out2, tokens, frozen_value_weight,
            after=into,
            in_specs=[WHOLE] * 11 + [HBM] * 2,
            out_specs=(HBM, WHOLE),
            scratch_shapes=[
                pltpu.VMEM((rows, 4 * span), BF16),
                pltpu.VMEM((2, rows, count), BF16),
                pltpu.VMEM((2, count, features), BF16),
                pltpu.VMEM((2, rows, count), BF16),
                pltpu.SemaphoreType.DMA((2, 2)),
                pltpu.SemaphoreType.DMA((2,)),
            ],
            input_output_aliases={13: 0} if into else {},
        )

    input_first, other_first = base(0, got_first, relay_first)
    input_gradient, other_second = base(first_rows, got_second, relay_second, input_first)
    crossed = call(mark_kernel, struct((8, 128), F32), after=(cross,), us=MARK_US)
    next_sum, mine_sum = call(
        near_kernel, (half_wide, struct((half, width), F32)),
        near_kept, got_near, cross, after=(up_away, other_first, relay_second, crossed), us=NEAR_US,
    )
    last = lax.ppermute(next_sum, "dp", swap(4))
    up_got = lax.ppermute(up_away, "fsdp", swap(2))
    up_mine, *up_sent = call(
        up_sum_kernel, (struct((half, features), F32),) + (struct((half, features), BF16),) * 3, up_keep, up_got,
        us=UP_US,
    )
    up_last = [lax.ppermute(sent, "dp", swap(4, k + 1)) for k, sent in enumerate(up_sent)]

    base_send, base_keep = call(share_kernel, (struct((rows, features), F32),) * 2, own_out, other_first, other_second, lora)
    base_got = lax.ppermute(base_send, "tp", swap(2))
    value_output, down_share, up_share = call(
        finish_kernel,
        (struct((rows, features), BF16), struct((half, width), F32), struct((half, features), F32)),
        base_keep, base_got, mine_sum, last, up_mine, *up_last, us=LAST_US,
    )
    shares = [share.reshape(jobs, rank // 2, share.shape[1]) for share in (down_share, up_share)]
    return value_output, input_gradient, *shares


def dispatch_rows(
    tokens,
    output_gradient,
    frozen_value_weight,
    adapter_down_weight,
    adapter_up_weight,
    deal,
    row_local_job,
):
    row_count = tokens.shape[0]
    width_half = tokens.shape[1]
    jobs_owned_here = adapter_down_weight.shape[0]
    rank_extent = adapter_down_weight.shape[1]
    partial_value_rows = adapter_up_weight.shape[2]
    partner_count = lax.axis_size("dp")
    job_slot_count = 5 * row_count // (4 * partner_count)
    slot_total = partner_count * job_slot_count
    tp_index = lax.axis_index("tp")
    grad_part = lax.dynamic_slice_in_dim(
        output_gradient, tp_index * partial_value_rows, partial_value_rows, 1
    )
    contract_last = (((1,), (1,)), ((), ()))
    full_weight = lax.all_gather(frozen_value_weight, "fsdp", axis=1, tiled=True)
    frozen_output = jnp.dot(tokens, full_weight, preferred_element_type=jnp.float32)
    frozen_gradient = lax.dot_general(
        output_gradient, full_weight, contract_last, preferred_element_type=jnp.float32
    )
    value_share = lax.psum_scatter(frozen_output, "tp", scatter_dimension=1, tiled=True)
    row_dest = deal[:, 0]
    dest_onehot = (row_dest[:, None] == jnp.arange(partner_count, dtype=jnp.int32)[None, :]).astype(
        jnp.int32
    )
    earlier = jnp.cumsum(dest_onehot, axis=0) - dest_onehot
    slot_rank = jnp.sum(earlier * dest_onehot, axis=1)
    row_slot = row_dest * job_slot_count + slot_rank
    row_ids = jnp.arange(row_count, dtype=jnp.int32)
    slot_full = jnp.zeros((slot_total,), jnp.int32).at[row_slot].set(1)
    source_row = jnp.zeros((slot_total,), jnp.int32).at[row_slot].set(row_ids)
    is_full = slot_full > 0
    send_tokens = jnp.where(is_full[:, None], tokens[source_row], jnp.zeros((), jnp.bfloat16))
    send_grads = jnp.where(is_full[:, None], grad_part[source_row], jnp.zeros((), jnp.bfloat16))
    send_jobs = jnp.where(is_full, row_local_job[source_row], -1)
    got_tokens, got_grads, got_jobs = (
        lax.all_to_all(
            send_tokens.reshape(partner_count, job_slot_count, width_half),
            "dp",
            split_axis=0,
            concat_axis=0,
            tiled=True,
        ),
        lax.all_to_all(
            send_grads.reshape(partner_count, job_slot_count, partial_value_rows),
            "dp",
            split_axis=0,
            concat_axis=0,
            tiled=True,
        ),
        lax.all_to_all(
            send_jobs.reshape(partner_count, job_slot_count),
            "dp",
            split_axis=0,
            concat_axis=0,
            tiled=True,
        ),
    )
    got_tokens = got_tokens.reshape(slot_total, width_half)
    got_grads = got_grads.reshape(slot_total, partial_value_rows)
    got_jobs = got_jobs.reshape(slot_total)
    job_pick = got_jobs[:, None] == jnp.arange(jobs_owned_here, dtype=jnp.int32)[None, :]
    flat_down_weight = adapter_down_weight.reshape(jobs_owned_here * rank_extent, width_half)
    flat_up_weight = adapter_up_weight.reshape(jobs_owned_here * rank_extent, partial_value_rows)
    every_down = lax.dot_general(
        got_tokens, flat_down_weight, contract_last, preferred_element_type=jnp.float32
    )
    every_up = lax.dot_general(
        got_grads, flat_up_weight, contract_last, preferred_element_type=jnp.float32
    )
    pick_mask = job_pick.astype(jnp.float32)[:, :, None]
    low_partial = jnp.sum(
        every_down.reshape(slot_total, jobs_owned_here, rank_extent) * pick_mask, axis=1
    )
    grad_partial = jnp.sum(
        every_up.reshape(slot_total, jobs_owned_here, rank_extent) * pick_mask, axis=1
    )
    low_rank, grad_rank = lax.psum((low_partial, grad_partial), "tp")
    pick_narrow = job_pick.astype(jnp.bfloat16)[:, :, None]
    wide_rank_rows = (pick_narrow * low_rank.astype(jnp.bfloat16)[:, None, :]).reshape(
        slot_total, jobs_owned_here * rank_extent
    )
    wide_gradient = (pick_narrow * grad_rank.astype(jnp.bfloat16)[:, None, :]).reshape(
        slot_total, jobs_owned_here * rank_extent
    )
    adapter_output = (
        ADAPTER_SCALE * jnp.dot(wide_rank_rows, flat_up_weight, preferred_element_type=jnp.float32)
    ).astype(jnp.bfloat16)
    adapter_gradient = (
        ADAPTER_SCALE * jnp.dot(wide_gradient, flat_down_weight, preferred_element_type=jnp.float32)
    ).astype(jnp.bfloat16)
    contract_first = (((0,), (0,)), ((), ()))
    down_product = ADAPTER_SCALE * lax.dot_general(
        wide_gradient, got_tokens, contract_first, preferred_element_type=jnp.float32
    )
    up_product = ADAPTER_SCALE * lax.dot_general(
        wide_rank_rows, got_grads, contract_first, preferred_element_type=jnp.float32
    )
    down_share, up_share = (
        lax.psum_scatter(
            down_product.reshape(jobs_owned_here, rank_extent, width_half),
            "fsdp",
            scatter_dimension=1,
            tiled=True,
        ),
        lax.psum_scatter(
            up_product.reshape(jobs_owned_here, rank_extent, partial_value_rows),
            "fsdp",
            scatter_dimension=1,
            tiled=True,
        ),
    )
    back_out, back_grad = (
        lax.all_to_all(
            adapter_output.reshape(partner_count, job_slot_count, partial_value_rows),
            "dp",
            split_axis=0,
            concat_axis=0,
            tiled=True,
        ),
        lax.all_to_all(
            adapter_gradient.reshape(partner_count, job_slot_count, width_half),
            "dp",
            split_axis=0,
            concat_axis=0,
            tiled=True,
        ),
    )
    row_out = back_out.reshape(slot_total, partial_value_rows)[row_slot]
    row_grad = back_grad.reshape(slot_total, width_half)[row_slot]
    value_output = (value_share + row_out.astype(jnp.float32)).astype(jnp.bfloat16)
    input_gradient = (frozen_gradient + row_grad.astype(jnp.float32)).astype(jnp.bfloat16)
    return (value_output, input_gradient, down_share, up_share)


def solution(mesh):
    small = dict(mesh.shape) == {"rep": 2, "dp": 4, "fsdp": 2, "tp": 2}
    local = gather_adapters if small else dispatch_rows
    in_specs = (
        P(("rep", "dp", "fsdp"), "tp"),
        P(("rep", "dp", "fsdp"), None),
        P("tp", "fsdp"),
        P(("rep", "dp"), None, "tp"),
        P(("rep", "dp"), None, "tp"),
        P(("rep", "dp", "fsdp"), None),
        P(("rep", "dp", "fsdp")),
    )
    out_specs = (
        P(("rep", "dp", "fsdp"), "tp"),
        P(("rep", "dp", "fsdp"), "tp"),
        P(("rep", "dp"), "fsdp", "tp"),
        P(("rep", "dp"), "fsdp", "tp"),
    )
    return jax.shard_map(local, mesh=mesh, in_specs=in_specs, out_specs=out_specs, check_vma=False)
```

```python
import functools

import jax
import jax.numpy as jnp
from jax import lax
from jax.experimental import pallas as pl
from jax.experimental.pallas import tpu as pltpu
from jax.sharding import PartitionSpec as P

ADAPTER_SCALE = 2.0

BF16 = jnp.bfloat16
F32 = jnp.float32
PLAIN = (((1,), (0,)), ((), ()))
CONTRACT_LAST = (((1,), (1,)), ((), ()))
VMEM_BYTES = 10 * 1024 * 1024
COLUMNS = 1024
OWN_PARTS = 4
PART_US = 3.6
SEND_US = 6
FAR_US = 6
SUM_US = 6
NEAR_US = 6
UP_US = 4
LAST_US = 15
MARK_US = 3
FIRST_SHARE = 4
WHOLE = pl.BlockSpec(memory_space=pltpu.VMEM)
ANY = pl.BlockSpec(memory_space=pl.ANY)
HBM = pl.BlockSpec(memory_space=pltpu.HBM)


def swap(extent, flip=1):
    return [(i, i ^ flip) for i in range(extent)]


def dot(left, right, dims=PLAIN):
    return lax.dot_general(left, right, dims, preferred_element_type=F32)


def struct(shape, dtype):
    return jax.ShapeDtypeStruct(shape, dtype)


def holders():
    here = lax.axis_index("dp")
    return here, here ^ 1, jnp.where(here < 2, 2, 1), jnp.where(here < 2, 3, 0)


def job_mask(span, rank, job_row):
    return lax.broadcasted_iota(jnp.int32, (span, job_row.shape[1]), 0) // rank == job_row


def prepare_kernel(gradient, deal, job, up, down, *refs):
    features = up.shape[1]
    start = pl.multiple_of(lax.axis_index("tp") * features, features)
    sources = gradient.at[:, pl.ds(start, features)], deal, job, up
    copies = [pltpu.make_async_copy(source, out, refs[4].at[k]) for k, (source, out) in enumerate(zip(sources, refs))]
    for copy in copies:
        copy.start()
    for copy in copies:
        copy.wait()


def grad_partial_kernel(rank, near, far, gradient, deal, job, out):
    here = lax.axis_index("dp")
    span = out.shape[0]
    part = gradient[...]
    owner = deal[...]
    total = jnp.zeros(out.shape, F32)
    for k in range(4):
        block = (near, far)[k // 2][k % 2 * span : (k % 2 + 1) * span]
        total += jnp.where(owner == (here ^ k), dot(block, part, CONTRACT_LAST), 0.0)
    out[...] = jnp.where(job_mask(span, rank, job[...]), total, 0.0)


def each_column(ref):
    def run(body):
        def step(i, carry):
            body(pl.ds(pl.multiple_of(i * COLUMNS, COLUMNS), COLUMNS))
            return carry

        lax.fori_loop(0, ref.shape[1] // COLUMNS, step, 0)

    return run


def half_rows(narrow, rank, which):
    half = rank // 2
    pick = [narrow[j * half : (j + 1) * half] for j in range(narrow.shape[0] // half)]
    low, high = jnp.concatenate(pick[0::2]), jnp.concatenate(pick[1::2])
    return jnp.where(which == 0, low, high)


def wide_rows(narrow, owner, names):
    return jnp.concatenate([jnp.where(owner == name, narrow, 0.0) for name in names]).astype(BF16)


def grad_send_kernel(rank, first, second, deal, tokens, rank_out, far_out, near_out):
    total = first[...] + second[...]
    rank_out[...] = total.astype(BF16)
    total = total.astype(BF16).astype(F32)
    sent = ADAPTER_SCALE * half_rows(total, rank, 1 - lax.axis_index("fsdp"))
    mine, beside, middle, end = holders()
    wide = wide_rows(sent, deal[...], (end, middle, beside, mine))
    split = far_out.shape[0]

    @each_column(tokens)
    def _(at):
        made = dot(wide, tokens[:, at])
        far_out[:, at] = made[:split].astype(BF16)
        near_out[:, at] = made[split:].astype(BF16)


def kept_rows(rank, grad_rank):
    return ADAPTER_SCALE * half_rows(grad_rank[...].astype(F32), rank, lax.axis_index("fsdp"))


def in_middle():
    here = lax.axis_index("dp")
    return (here == 1) | (here == 2)


def far_kernel(rank, got, grad_rank, deal, tokens, down_cross, out, swap_out):
    _, _, middle, end = holders()
    wide = wide_rows(kept_rows(rank, grad_rank), deal[...], (end, middle))

    @each_column(tokens)
    def _(at):
        made = (dot(wide, tokens[:, at]) + got[:, at].astype(F32)).astype(BF16)
        out[:, at] = made
        swap_out[:, at] = jnp.where(in_middle(), down_cross[:, at], made)


def near_kept_kernel(rank, grad_rank, deal, tokens, out):
    mine, beside, _, _ = holders()
    wide = wide_rows(kept_rows(rank, grad_rank), deal[...], (beside, mine))

    @each_column(tokens)
    def _(at):
        out[:, at] = dot(wide, tokens[:, at])


def near_kernel(kept, got, cross, next_out, mine_out):
    split = next_out.shape[0]

    @each_column(kept)
    def _(at):
        made = kept[:, at] + got[:, at].astype(F32) + cross[:, at].astype(F32)
        next_out[:, at] = made[:split].astype(BF16)
        mine_out[:, at] = made[split:]


def low_kernel(rank, names, blocks, *refs):
    tokens, deal, job = refs[:3]
    out = refs[-1]
    owner = deal[...]
    name = holders()
    started = len(refs) - 4 > sum(blocks)
    out[...] = jnp.zeros(out.shape, F32)

    @each_column(tokens)
    def _(at):
        left = list(refs[3:-1])
        total = out[...]
        for k, count in zip(names, blocks):
            block = left.pop(0)[:, at]
            if count == 2:
                block = jnp.where(in_middle(), block, left.pop(0)[:, at])
            total += jnp.where(owner == name[k], dot(block, tokens[:, at], CONTRACT_LAST), 0.0)
        out[...] = total

    out[...] = jnp.where(job_mask(out.shape[0], rank, job[...]), out[...], 0.0)
    if started:
        out[...] += refs[-2][...]


def up_kernel(rank, low, low_got, gradient, deal, near, far, keep_out, away_out, lora_out):
    here = lax.axis_index("dp")
    span = low.shape[0]
    half = span // 2
    narrow = (low[...] + low_got[...]).astype(BF16).astype(F32)
    owner = deal[...]
    part = gradient[...]
    wide = jnp.concatenate([jnp.where(owner == (here ^ k), narrow, 0.0) for k in range(4)])
    made = ADAPTER_SCALE * dot(wide.astype(BF16), part)
    side = lax.axis_index("fsdp")
    for k in range(4):
        block = made[k * span : (k + 1) * span]
        keep_out[k * half : (k + 1) * half] = half_rows(block, rank, side)
        away_out[k * half : (k + 1) * half] = half_rows(block, rank, 1 - side).astype(BF16)
    ups = jnp.concatenate([near[...], far[...]])
    lora_out[...] = ADAPTER_SCALE * dot(wide.T.astype(BF16), ups)


def up_sum_kernel(keep, got, mine, *sent):
    total = keep[...] + got[...].astype(F32)
    half = mine.shape[0]
    mine[...] = total[:half]
    for k, out in enumerate(sent):
        out[...] = total[(k + 1) * half : (k + 2) * half].astype(BF16)


def own_kernel(tokens, own, out, buffer, sems):
    count = own.shape[0] // OWN_PARTS
    copies = []
    for k in range(OWN_PARTS):
        at = pl.ds(k * count, count)
        copies.append(pltpu.make_async_copy(own.at[at], buffer.at[at], sems.at[k]))
        copies[-1].start()
    for k, copy in enumerate(copies):
        at = pl.ds(k * count, count)
        copy.wait()
        part = dot(tokens[:, at], buffer[at])
        out[...] = part if k == 0 else out[...] + part


def base_kernel(offset, gradient, grad_rank, deal, direct, relayed, *refs):
    downs, (tokens, own) = refs[:6], refs[6:8]
    grad_out, other_out, wide, buffer, own_in, token_in, sems, out_sems = refs[-8:]
    features = own.shape[1]
    count = direct.shape[0]
    mine = pl.multiple_of(lax.axis_index("fsdp") * features, features)
    other = pl.multiple_of((1 - lax.axis_index("fsdp")) * features, features)
    rep = lax.axis_index("rep")
    spots, copies, stores = [], [], []
    for side in range(2):
        start = (rep ^ side) * (own.shape[0] // 2) + offset
        spots.append(pl.ds(pl.multiple_of(start, 256), count))
        copies.append(
            [
                pltpu.make_async_copy(own.at[spots[side], :], own_in.at[side], sems.at[side, 0]),
                pltpu.make_async_copy(tokens.at[:, spots[side]], token_in.at[side], sems.at[side, 1]),
            ]
        )
        for copy in copies[side]:
            copy.start()
    narrow = ADAPTER_SCALE * grad_rank[...].astype(F32)
    wide[...] = jnp.concatenate([jnp.where(deal[...] == name, narrow, 0.0) for name in holders()]).T.astype(BF16)
    for side, (at, weight) in enumerate(zip(spots, (direct, relayed))):
        parts = [down[:, at] for down in downs]
        parts[2:] = [jnp.where(in_middle(), parts[k], parts[k + 1]) for k in (2, 4)]
        total = dot(wide[...], jnp.concatenate(parts))
        total += dot(gradient[:, pl.ds(other, features)], weight[...], CONTRACT_LAST)
        copies[side][0].wait()
        total += dot(gradient[:, pl.ds(mine, features)], own_in[side], CONTRACT_LAST)
        buffer[side] = total.astype(BF16)
        stores.append(pltpu.make_async_copy(buffer.at[side], grad_out.at[:, at], out_sems.at[side]))
        stores[side].start()
        copies[side][1].wait()
        other_part = dot(token_in[side], weight[...])
        other_out[...] = other_part if side == 0 else other_out[...] + other_part
    for store in stores:
        store.wait()


def call(kernel, out_shape, *args, after=(), in_specs=None, out_specs=None, us=0, **more):
    count = len(args)
    if out_specs is None:
        out_specs = (WHOLE,) * len(out_shape) if isinstance(out_shape, tuple) else WHOLE
    if after:
        inner = kernel
        kernel = lambda *refs: inner(*refs[:count], *refs[count + len(after) :])
    return pl.pallas_call(
        kernel,
        out_shape=out_shape,
        in_specs=(in_specs or [WHOLE] * count) + [ANY] * len(after),
        out_specs=out_specs,
        compiler_params=pltpu.CompilerParams(vmem_limit_bytes=VMEM_BYTES),
        cost_estimate=pl.CostEstimate(flops=int(us * 1.15e9), bytes_accessed=0, transcendentals=0) if us else None,
        **more,
    )(*args, *after)


def cut_kernel(weight, first, second, sems):
    half = weight.shape[0] // 2
    start = pl.multiple_of(lax.axis_index("rep") * half, half)
    count = first.shape[0]
    copies = [
        pltpu.make_async_copy(weight.at[pl.ds(start, count)], first, sems.at[0]),
        pltpu.make_async_copy(weight.at[pl.ds(start + count, half - count)], second, sems.at[1]),
    ]
    for copy in copies:
        copy.start()
    for copy in copies:
        copy.wait()


def join_kernel(one, two, out):
    half = one.shape[0]
    out[:half] = one[...]
    out[half:] = two[...]


def share_kernel(own, first, second, lora, send_out, keep_out):
    other = first[...] + second[...]
    same = lax.axis_index("fsdp") == lax.axis_index("tp")
    send_out[...] = jnp.where(same, other, own[...])
    keep_out[...] = jnp.where(same, own[...], other) + lora[...]


def total_kernel(*refs):
    total = refs[0][...]
    for ref in refs[1:-1]:
        total += ref[...].astype(F32)
    refs[-1][...] = total.astype(refs[-1].dtype)


def finish_kernel(base_keep, base_got, mine, last, up_mine, one, two, three, value_out, down_out, up_out):
    total_kernel(base_keep, base_got, value_out)
    total_kernel(up_mine, one, two, three, up_out)
    down_out[...] = mine[...] + last[...].astype(F32)


def mark_kernel(out):
    out[...] = jnp.zeros(out.shape, out.dtype)


def add_kernel(one, two, out):
    out[...] = (one[...].astype(F32) + two[...].astype(F32)).astype(BF16)


def ordered(value, before):
    return lax.optimization_barrier((value, before))[0]


def gather_adapters(
    tokens,
    output_gradient,
    frozen_value_weight,
    adapter_down_weight,
    adapter_up_weight,
    deal,
    row_local_job,
):
    rows, width = tokens.shape
    jobs, rank, features = adapter_up_weight.shape
    span = jobs * rank
    half = span // 2
    down = adapter_down_weight.reshape(span, width)
    up = adapter_up_weight.reshape(span, features)
    deal = deal.reshape(1, rows)
    job = row_local_job.reshape(1, rows)
    first_rows = width * FIRST_SHARE // 16
    outward, middle = [(1, 0), (2, 3)], [(1, 2), (2, 1)]

    up_got_first = lax.ppermute(up, "dp", swap(4))
    row = struct((1, rows), jnp.int32)
    grad_mine, deal, job, up = call(
        prepare_kernel, (struct((rows, features), BF16), row, row, struct((span, features), BF16)),
        output_gradient, deal, job, up, down,
        in_specs=[ANY] * 4 + [WHOLE], scratch_shapes=[pltpu.SemaphoreType.DMA((4,))],
    )
    up_pair = call(join_kernel, struct((2 * span, features), BF16), up, up_got_first, after=(grad_mine,))
    ups = up_pair, lax.ppermute(up_pair, "dp", swap(4, 2))
    weight_first, weight_second = call(
        cut_kernel,
        (struct((first_rows, features), BF16), struct((width // 2 - first_rows, features), BF16)),
        frozen_value_weight,
        in_specs=[HBM],
        out_specs=(ANY, ANY),
        scratch_shapes=[pltpu.SemaphoreType.DMA((2,))],
    )
    got_first = lax.ppermute(weight_first, "fsdp", swap(2))

    narrow = struct((span, rows), F32)
    half_wide = struct((half, width), BF16)
    span_wide = struct((span, width), BF16)
    grad_part = call(functools.partial(grad_partial_kernel, rank), narrow, *ups, grad_mine, deal, job, us=PART_US)
    grad_got = lax.ppermute(grad_part, "tp", swap(2))
    grad_rank, send_far, send_near = call(
        functools.partial(grad_send_kernel, rank), (struct((span, rows), BF16), span_wide, span_wide),
        grad_part, grad_got, deal, tokens, after=(got_first,), us=SEND_US,
    )
    down_sent = ordered(down, grad_part)
    down_next = lax.ppermute(down_sent, "dp", swap(4))
    down_cross = lax.ppermute(ordered(down, grad_part), "dp", middle)
    got_far = lax.ppermute(send_far, "fsdp", swap(2))
    own_out = call(
        own_kernel,
        struct((rows, features), F32),
        tokens,
        frozen_value_weight,
        after=(send_far,),
        in_specs=[WHOLE, HBM],
        scratch_shapes=[pltpu.VMEM((width, features), BF16), pltpu.SemaphoreType.DMA((OWN_PARTS,))],
    )
    relay_first = lax.ppermute(ordered(got_first, own_out), "rep", swap(2))
    near_kept = call(
        functools.partial(near_kept_kernel, rank), struct((span, width), F32), grad_rank, deal, tokens
    )
    far, far_swap = call(
        functools.partial(far_kernel, rank), (span_wide, span_wide),
        got_far, grad_rank, deal, tokens, down_cross, after=(own_out, down_next, near_kept), us=FAR_US,
    )
    got_second = lax.ppermute(ordered(weight_second, got_far), "fsdp", swap(2))
    swapped = lax.ppermute(far_swap, "dp", swap(4))
    down_cross2 = lax.ppermute(ordered(down_next, down_cross), "dp", middle)
    low_near = call(
        functools.partial(low_kernel, rank, (0, 1), (1, 1)),
        narrow, tokens, deal, job, down, down_next, after=(far,),
    )
    low_first = call(
        functools.partial(low_kernel, rank, (2,), (2,)),
        narrow, tokens, deal, job, down_cross, swapped, low_near,
    )
    far_sum = call(add_kernel, span_wide, far, swapped, after=(down_cross2, low_near, relay_first), us=SUM_US)
    got_near = lax.ppermute(ordered(send_near, far), "fsdp", swap(2))
    cross = lax.ppermute(far_sum, "dp", middle)
    down_out2 = lax.ppermute(ordered(down_cross2, far), "dp", outward)
    relay_second = lax.ppermute(ordered(got_second, far_sum), "rep", swap(2))
    low_part = call(
        functools.partial(low_kernel, rank, (3,), (2,)), narrow, tokens, deal, job, down_cross2, down_out2, low_first, after=()
    )
    low_got = lax.ppermute(low_part, "tp", swap(2))
    up_half = struct((4 * half, features), F32), struct((4 * half, features), BF16)
    up_keep, up_away, lora = call(
        functools.partial(up_kernel, rank), (*up_half, struct((rows, features), F32)),
        low_part, low_got, grad_mine, deal, *ups,
    )
    def base(offset, direct, relayed, *into):
        count = direct.shape[0]
        return call(
            functools.partial(base_kernel, offset),
            (struct((rows, width), BF16), struct((rows, features), F32)),
            output_gradient, grad_rank, deal, direct, relayed,
            down, down_next, down_cross, swapped, down_cross2, down_out2, tokens, frozen_value_weight,
            after=into,
            in_specs=[WHOLE] * 11 + [HBM] * 2,
            out_specs=(HBM, WHOLE),
            scratch_shapes=[
                pltpu.VMEM((rows, 4 * span), BF16),
                pltpu.VMEM((2, rows, count), BF16),
                pltpu.VMEM((2, count, features), BF16),
                pltpu.VMEM((2, rows, count), BF16),
                pltpu.SemaphoreType.DMA((2, 2)),
                pltpu.SemaphoreType.DMA((2,)),
            ],
            input_output_aliases={13: 0} if into else {},
        )

    input_first, other_first = base(0, got_first, relay_first)
    input_gradient, other_second = base(first_rows, got_second, relay_second, input_first)
    crossed = call(mark_kernel, struct((8, 128), F32), after=(cross,), us=MARK_US)
    next_sum, mine_sum = call(
        near_kernel, (half_wide, struct((half, width), F32)),
        near_kept, got_near, cross, after=(relay_second, crossed), us=NEAR_US,
    )
    last = lax.ppermute(next_sum, "dp", swap(4))
    up_got = lax.ppermute(up_away, "fsdp", swap(2))
    up_mine, *up_sent = call(
        up_sum_kernel, (struct((half, features), F32),) + (struct((half, features), BF16),) * 3, up_keep, up_got,
        us=UP_US,
    )
    up_last = [lax.ppermute(sent, "dp", swap(4, k + 1)) for k, sent in enumerate(up_sent)]

    base_send, base_keep = call(share_kernel, (struct((rows, features), F32),) * 2, own_out, other_first, other_second, lora)
    base_got = lax.ppermute(base_send, "tp", swap(2))
    value_output, down_share, up_share = call(
        finish_kernel,
        (struct((rows, features), BF16), struct((half, width), F32), struct((half, features), F32)),
        base_keep, base_got, mine_sum, last, up_mine, *up_last, us=LAST_US,
    )
    shares = [share.reshape(jobs, rank // 2, share.shape[1]) for share in (down_share, up_share)]
    return value_output, input_gradient, *shares


def dispatch_rows(
    tokens,
    output_gradient,
    frozen_value_weight,
    adapter_down_weight,
    adapter_up_weight,
    deal,
    row_local_job,
):
    row_count = tokens.shape[0]
    width_half = tokens.shape[1]
    jobs_owned_here = adapter_down_weight.shape[0]
    rank_extent = adapter_down_weight.shape[1]
    partial_value_rows = adapter_up_weight.shape[2]
    partner_count = lax.axis_size("dp")
    job_slot_count = 5 * row_count // (4 * partner_count)
    slot_total = partner_count * job_slot_count
    tp_index = lax.axis_index("tp")
    grad_part = lax.dynamic_slice_in_dim(
        output_gradient, tp_index * partial_value_rows, partial_value_rows, 1
    )
    contract_last = (((1,), (1,)), ((), ()))
    full_weight = lax.all_gather(frozen_value_weight, "fsdp", axis=1, tiled=True)
    frozen_output = jnp.dot(tokens, full_weight, preferred_element_type=jnp.float32)
    frozen_gradient = lax.dot_general(
        output_gradient, full_weight, contract_last, preferred_element_type=jnp.float32
    )
    value_share = lax.psum_scatter(frozen_output, "tp", scatter_dimension=1, tiled=True)
    row_dest = deal[:, 0]
    dest_onehot = (row_dest[:, None] == jnp.arange(partner_count, dtype=jnp.int32)[None, :]).astype(
        jnp.int32
    )
    earlier = jnp.cumsum(dest_onehot, axis=0) - dest_onehot
    slot_rank = jnp.sum(earlier * dest_onehot, axis=1)
    row_slot = row_dest * job_slot_count + slot_rank
    row_ids = jnp.arange(row_count, dtype=jnp.int32)
    slot_full = jnp.zeros((slot_total,), jnp.int32).at[row_slot].set(1)
    source_row = jnp.zeros((slot_total,), jnp.int32).at[row_slot].set(row_ids)
    is_full = slot_full > 0
    send_tokens = jnp.where(is_full[:, None], tokens[source_row], jnp.zeros((), jnp.bfloat16))
    send_grads = jnp.where(is_full[:, None], grad_part[source_row], jnp.zeros((), jnp.bfloat16))
    send_jobs = jnp.where(is_full, row_local_job[source_row], -1)
    got_tokens, got_grads, got_jobs = (
        lax.all_to_all(
            send_tokens.reshape(partner_count, job_slot_count, width_half),
            "dp",
            split_axis=0,
            concat_axis=0,
            tiled=True,
        ),
        lax.all_to_all(
            send_grads.reshape(partner_count, job_slot_count, partial_value_rows),
            "dp",
            split_axis=0,
            concat_axis=0,
            tiled=True,
        ),
        lax.all_to_all(
            send_jobs.reshape(partner_count, job_slot_count),
            "dp",
            split_axis=0,
            concat_axis=0,
            tiled=True,
        ),
    )
    got_tokens = got_tokens.reshape(slot_total, width_half)
    got_grads = got_grads.reshape(slot_total, partial_value_rows)
    got_jobs = got_jobs.reshape(slot_total)
    job_pick = got_jobs[:, None] == jnp.arange(jobs_owned_here, dtype=jnp.int32)[None, :]
    flat_down_weight = adapter_down_weight.reshape(jobs_owned_here * rank_extent, width_half)
    flat_up_weight = adapter_up_weight.reshape(jobs_owned_here * rank_extent, partial_value_rows)
    every_down = lax.dot_general(
        got_tokens, flat_down_weight, contract_last, preferred_element_type=jnp.float32
    )
    every_up = lax.dot_general(
        got_grads, flat_up_weight, contract_last, preferred_element_type=jnp.float32
    )
    pick_mask = job_pick.astype(jnp.float32)[:, :, None]
    low_partial = jnp.sum(
        every_down.reshape(slot_total, jobs_owned_here, rank_extent) * pick_mask, axis=1
    )
    grad_partial = jnp.sum(
        every_up.reshape(slot_total, jobs_owned_here, rank_extent) * pick_mask, axis=1
    )
    low_rank, grad_rank = lax.psum((low_partial, grad_partial), "tp")
    pick_narrow = job_pick.astype(jnp.bfloat16)[:, :, None]
    wide_rank_rows = (pick_narrow * low_rank.astype(jnp.bfloat16)[:, None, :]).reshape(
        slot_total, jobs_owned_here * rank_extent
    )
    wide_gradient = (pick_narrow * grad_rank.astype(jnp.bfloat16)[:, None, :]).reshape(
        slot_total, jobs_owned_here * rank_extent
    )
    adapter_output = (
        ADAPTER_SCALE * jnp.dot(wide_rank_rows, flat_up_weight, preferred_element_type=jnp.float32)
    ).astype(jnp.bfloat16)
    adapter_gradient = (
        ADAPTER_SCALE * jnp.dot(wide_gradient, flat_down_weight, preferred_element_type=jnp.float32)
    ).astype(jnp.bfloat16)
    contract_first = (((0,), (0,)), ((), ()))
    down_product = ADAPTER_SCALE * lax.dot_general(
        wide_gradient, got_tokens, contract_first, preferred_element_type=jnp.float32
    )
    up_product = ADAPTER_SCALE * lax.dot_general(
        wide_rank_rows, got_grads, contract_first, preferred_element_type=jnp.float32
    )
    down_share, up_share = (
        lax.psum_scatter(
            down_product.reshape(jobs_owned_here, rank_extent, width_half),
            "fsdp",
            scatter_dimension=1,
            tiled=True,
        ),
        lax.psum_scatter(
            up_product.reshape(jobs_owned_here, rank_extent, partial_value_rows),
            "fsdp",
            scatter_dimension=1,
            tiled=True,
        ),
    )
    back_out, back_grad = (
        lax.all_to_all(
            adapter_output.reshape(partner_count, job_slot_count, partial_value_rows),
            "dp",
            split_axis=0,
            concat_axis=0,
            tiled=True,
        ),
        lax.all_to_all(
            adapter_gradient.reshape(partner_count, job_slot_count, width_half),
            "dp",
            split_axis=0,
            concat_axis=0,
            tiled=True,
        ),
    )
    row_out = back_out.reshape(slot_total, partial_value_rows)[row_slot]
    row_grad = back_grad.reshape(slot_total, width_half)[row_slot]
    value_output = (value_share + row_out.astype(jnp.float32)).astype(jnp.bfloat16)
    input_gradient = (frozen_gradient + row_grad.astype(jnp.float32)).astype(jnp.bfloat16)
    return (value_output, input_gradient, down_share, up_share)


def solution(mesh):
    small = dict(mesh.shape) == {"rep": 2, "dp": 4, "fsdp": 2, "tp": 2}
    local = gather_adapters if small else dispatch_rows
    in_specs = (
        P(("rep", "dp", "fsdp"), "tp"),
        P(("rep", "dp", "fsdp"), None),
        P("tp", "fsdp"),
        P(("rep", "dp"), None, "tp"),
        P(("rep", "dp"), None, "tp"),
        P(("rep", "dp", "fsdp"), None),
        P(("rep", "dp", "fsdp")),
    )
    out_specs = (
        P(("rep", "dp", "fsdp"), "tp"),
        P(("rep", "dp", "fsdp"), "tp"),
        P(("rep", "dp"), "fsdp", "tp"),
        P(("rep", "dp"), "fsdp", "tp"),
    )
    return jax.shard_map(local, mesh=mesh, in_specs=in_specs, out_specs=out_specs, check_vma=False)
```
